256 devices in a mesh: row: 16 (over x, y_hi, core), col: 16 (over z, y_lo).
Axes of the slice: x: 4, y: 4 (y_hi: 2, y_lo: 2; y = y_hi * 2 + y_lo), z: 8, core: 2. Of those that a mesh axis runs over, the one named last changes fastest.
Arguments:
- features: bfloat16 [65536, 128], P(('row', 'col')), may hold values from -6 to 6
- cotangent: bfloat16 [65536, 256], P(('row', 'col')), may hold values from -6 to 6
- w_self: bfloat16 [128, 256], replicated, may hold values from -0.5 to 0.5
- w_neigh: bfloat16 [128, 256], replicated, may hold values from -0.5 to 0.5
- adj_blocks: bfloat16 [16, 16, 80, 128, 128], P('row', 'col'), may hold values from 0 to 1
- block_rows: int32 [16, 16, 80], P('row', 'col'), may hold values from 0 to 31
- block_cols: int32 [16, 16, 80], P('row', 'col'), may hold values from 0 to 31
- block_count: int32 [16, 16], P('row', 'col'), may hold values from 20 to 80, as said below
Outputs:
- grad_features: float32 [65536, 128], P(('row', 'col'))
- grad_self: float32 [128, 256], replicated
- grad_neigh: float32 [128, 256], replicated
The draws below stay inside these ranges and needn't reach their ends.
Inputs may be any that keep to these rules, and one draw needn't show every extreme that they name: `block_count`: every device has at least a quarter of 80 used slots, and at least one device uses all 80.
All inputs are finite; a program needn't handle non-finite values.
Results may differ from the reference program's by a relative error of at most 0.0047.
Values may be sent and summed in bfloat16 or wider, within the bound.
No kernel may reach another device: no remote copies, remote signals or barrier semaphores. Data moves between devices by JAX's collectives and lax.ppermute only.
A program may use at most 64 MiB of HBM per device.

```python
import jax
import jax.numpy as jnp
from jax import lax

F = 128
H = 256
BLK = 128
NODE_DEV = 256
NB_MAX = 80
NODES = 65536
N_ROW = 16
N_COL = 16


def draw_block_count(key, part):
    key = jax.random.fold_in(key, 11)
    first, second = jax.random.split(key)
    divisor = jax.random.randint(first, (N_ROW * N_COL,), 1, 5)
    counts = NB_MAX // divisor
    spot = jax.random.randint(second, (), 0, N_ROW * N_COL)
    counts = counts.at[spot].set(NB_MAX)
    return counts.reshape(N_ROW, N_COL).astype(jnp.int32)


def touch_ends(drawn, rng, least, top_value):
    spot = [jax.random.randint(jax.random.fold_in(rng, axis), (), 0, length) for axis, length in enumerate(drawn.shape)]
    main_axis = drawn.shape.index(max(drawn.shape))
    next_to = spot[:main_axis] + [(spot[main_axis] + 1) % drawn.shape[main_axis]] + spot[main_axis + 1:]
    return drawn.at[tuple(spot)].set(least).at[tuple(next_to)].set(top_value)


def block_scale(own_key, extent, cuts, least, top_value):
    gain = 1.0
    for axis_at, shards_of in cuts:
        draws = jax.random.uniform(jax.random.fold_in(jax.random.fold_in(own_key, 6), axis_at), (shards_of,), jnp.float32, least / len(cuts), top_value / len(cuts))
        gain = gain * jnp.repeat(jnp.exp(draws), extent[axis_at] // shards_of).reshape((-1,) + (1,) * (len(extent) - 1 - axis_at))
    return gain


def centred(own_key, shape, deviation, bound, pieces=(), kind=jnp.bfloat16):
    gain = block_scale(own_key, shape, pieces, -0.22, 0.18) if pieces else 1.0
    entries = jax.random.normal(own_key, shape, jnp.float32) * deviation * gain
    return jnp.minimum(jnp.maximum(entries, -bound), bound).astype(kind)


def setup_inputs(seed: int = 0) -> dict:
    seeds = jax.random.split(jax.random.key(seed), 9)
    features = centred(seeds[0], (NODES, F), 1.0, 6.0, ((0, 256),))
    cotangent = centred(seeds[1], (NODES, H), 1.0, 6.0, ((0, 256),))
    w_self = centred(seeds[2], (F, H), F ** -0.5, 0.5)
    w_neigh = centred(seeds[3], (F, H), F ** -0.5, 0.5)
    adj_blocks = jnp.clip(1.0 * jax.random.uniform(seeds[4], (N_ROW, N_COL, NB_MAX, BLK, BLK), jnp.float32) ** block_scale(seeds[4], (N_ROW, N_COL, NB_MAX, BLK, BLK), ((0, 16), (1, 16)), -0.2, 0.2), 0.0, 1.0).astype(jnp.bfloat16)
    block_rows = touch_ends(jax.random.randint(seeds[5], (N_ROW, N_COL, NB_MAX), 0, N_COL * NODE_DEV // BLK), jax.random.fold_in(seeds[5], 1), 0, (N_COL * NODE_DEV // BLK) - 1).astype(jnp.int32)
    block_cols = touch_ends(jax.random.randint(seeds[6], (N_ROW, N_COL, NB_MAX), 0, N_ROW * NODE_DEV // BLK), jax.random.fold_in(seeds[6], 1), 0, (N_ROW * NODE_DEV // BLK) - 1).astype(jnp.int32)
    block_count = draw_block_count(jax.random.fold_in(seeds[8], 71), 0)
    return {"features": features, "cotangent": cotangent, "w_self": w_self, "w_neigh": w_neigh, "adj_blocks": adj_blocks, "block_rows": block_rows, "block_cols": block_cols, "block_count": block_count}


def dense_part(feats, cot, sums, degree, w_self, w_neigh):
    norm = lax.rsqrt(1.0 + degree)[:, None]
    agg = (sums * norm).astype(jnp.bfloat16)
    pre = jnp.dot(feats, w_self, preferred_element_type=jnp.float32) + jnp.dot(agg, w_neigh, preferred_element_type=jnp.float32)
    sig = jax.nn.sigmoid(pre)
    dz = (cot * (sig * (1.0 + pre * (1.0 - sig)))).astype(jnp.bfloat16)
    ds = (jnp.dot(dz, w_neigh.T, preferred_element_type=jnp.float32) * norm).astype(jnp.bfloat16)
    return (agg, dz, ds)

def reference(features, cotangent, w_self, w_neigh, adj_blocks, block_rows, block_cols, block_count):
    stripe_rows = N_COL * NODE_DEV
    stripe_cols = N_ROW * NODE_DEV
    grid = features.reshape(N_ROW, N_COL, NODE_DEV, F)
    slots = jnp.arange(NB_MAX, dtype=jnp.int32)
    devices = jnp.arange(N_ROW * N_COL, dtype=jnp.int32)

    def forward_step(carry, dev):
        sums, degs = carry
        rpos = dev // N_COL
        cpos = dev % N_COL
        col_feats = lax.dynamic_index_in_dim(grid, cpos, axis=1, keepdims=False).reshape(stripe_cols, F)
        blocks = adj_blocks[rpos, cpos].astype(jnp.float32)
        live = (slots < block_count[rpos, cpos]).astype(jnp.float32)
        picked = col_feats.reshape(-1, BLK, F)[block_cols[rpos, cpos]].astype(jnp.float32)
        prod = jnp.einsum('kij,kjf->kif', blocks, picked) * live[:, None, None]
        part = jax.ops.segment_sum(prod, block_rows[rpos, cpos], num_segments=stripe_rows // BLK).reshape(stripe_rows, F)
        weight = lax.optimization_barrier(jnp.sum(blocks, axis=2)) * live[:, None]
        pdeg = jax.ops.segment_sum(weight, block_rows[rpos, cpos], num_segments=stripe_rows // BLK).reshape(stripe_rows)
        return ((sums.at[rpos].add(part), degs.at[rpos].add(pdeg)), None)
    init = (jnp.zeros((N_ROW, stripe_rows, F), jnp.float32), jnp.zeros((N_ROW, stripe_rows), jnp.float32))
    (sums, degs), _ = lax.scan(forward_step, init, devices)
    sums = sums.reshape(NODES, F)
    degree = degs.reshape(NODES)
    agg, dz, ds = dense_part(features, cotangent, sums, degree, w_self, w_neigh)
    ds_grid = ds.reshape(N_ROW, stripe_rows, F)

    def adjoint_step(acc, dev):
        rpos = dev // N_COL
        cpos = dev % N_COL
        rows_here = lax.dynamic_index_in_dim(ds_grid, rpos, axis=0, keepdims=False)
        blocks = adj_blocks[rpos, cpos].astype(jnp.float32)
        live = (slots < block_count[rpos, cpos]).astype(jnp.float32)
        picked = rows_here.reshape(-1, BLK, F)[block_rows[rpos, cpos]].astype(jnp.float32)
        prod = jnp.einsum('kij,kif->kjf', blocks, picked) * live[:, None, None]
        part = jax.ops.segment_sum(prod, block_cols[rpos, cpos], num_segments=stripe_cols // BLK).reshape(stripe_cols, F)
        return (acc.at[cpos].add(part), None)
    acc, _ = lax.scan(adjoint_step, jnp.zeros((N_COL, stripe_cols, F), jnp.float32), devices)
    adjoint = acc.reshape(N_COL, N_ROW, NODE_DEV, F).transpose(1, 0, 2, 3).reshape(NODES, F)
    grad_features = jnp.dot(dz, w_self.T, preferred_element_type=jnp.float32) + adjoint
    scale = NODES ** (-0.5)
    grad_self = jnp.dot(features.T, dz, preferred_element_type=jnp.float32) * scale
    grad_neigh = jnp.dot(agg.T, dz, preferred_element_type=jnp.float32) * scale
    return (grad_features, grad_self, grad_neigh)
```

```python
import functools

import jax
import jax.numpy as jnp
from jax import lax
from jax.experimental import pallas as pl
from jax.experimental.pallas import tpu as pltpu
from jax.sharding import PartitionSpec as P

BLK = 128
N_AX = 16
BPD = 2
STRIPE = N_AX * BPD
UNROLL = 8
PIECE = 32
TAIL = 16
f32 = jnp.float32
bf16 = jnp.bfloat16

VMEM = pl.BlockSpec(memory_space=pltpu.VMEM)
SMEM = pl.BlockSpec(memory_space=pltpu.SMEM)
PARAMS = pltpu.CompilerParams(vmem_limit_bytes=24 * 1024 * 1024)


def dot(a, b, contract=((1,), (0,))):
    return lax.dot_general(a, b, (contract, ((), ())), preferred_element_type=f32)


def slots_loop(count_ref, index_ref, acc_ref, product):
    acc_ref[...] = jnp.zeros_like(acc_ref)
    count = count_ref[0, 0]

    def group(g, carry):
        base = g * UNROLL
        terms = [product(base + u) for u in range(UNROLL)]
        for u in range(UNROLL):
            k = base + u
            at = jnp.where(k < count, index_ref[0, k], STRIPE)
            acc_ref[at] += terms[u]
        return carry

    lax.fori_loop(0, (count + UNROLL - 1) // UNROLL, group, 0)


def degree_kernel(count_ref, rows_ref, adj_ref, out_ref, acc_ref):
    ones = jnp.ones((8, BLK), bf16)
    slots_loop(count_ref, rows_ref, acc_ref, lambda k: dot(ones, adj_ref[k], ((1,), (1,))))
    for d in range(N_AX):
        parts = [acc_ref[d * BPD + b][0:1] for b in range(BPD)]
        both = jnp.concatenate(parts + parts + [jnp.zeros((TAIL - 2 * BPD, BLK), f32)], axis=0)
        high = both.astype(bf16)
        low = (both - high.astype(f32)).astype(bf16)
        at = lax.broadcasted_iota(jnp.int32, (TAIL, BLK), 0)
        out_ref[d] = jnp.where(at < BPD, high.astype(f32), low.astype(f32)).astype(bf16)


def forward_kernel(count_ref, rows_ref, cols_ref, adj_ref, x_ref, deg_ref, out_ref, acc_ref):
    slots_loop(count_ref, rows_ref, acc_ref, lambda k: dot(adj_ref[k], x_ref[cols_ref[0, k]]))
    for d in range(N_AX):
        for b in range(BPD):
            out_ref[d, b * BLK : (b + 1) * BLK, :] = acc_ref[d * BPD + b].astype(bf16)
        out_ref[d, BPD * BLK :, :] = deg_ref[d]


def dense_kernel(got_ref, x_ref, cot_ref, ws_ref, wn_ref, out_ref, dz_ref):
    total = got_ref[0].astype(f32)
    for d in range(1, N_AX):
        total += got_ref[d].astype(f32)
    n = BPD * BLK
    degree = total[n : n + BPD] + total[n + BPD : n + 2 * BPD]
    norm_lanes = lax.rsqrt(1.0 + degree)
    norm = jnp.concatenate(
        [jnp.transpose(jnp.broadcast_to(norm_lanes[b : b + 1], (BLK, BLK))) for b in range(BPD)], axis=0
    )
    agg = (total[:n] * norm).astype(bf16)
    x = x_ref[...]
    pre = dot(x, ws_ref[...]) + dot(agg, wn_ref[...])
    sig = jax.nn.sigmoid(pre)
    dz = (cot_ref[...].astype(f32) * (sig * (1.0 + pre * (1.0 - sig)))).astype(bf16)
    dz_ref[...] = dz
    ds = dot(dz, wn_ref[...], ((1,), (1,))) * norm
    grads = jnp.concatenate([dot(x, dz, ((0,), (0,))), dot(agg, dz, ((0,), (0,)))], axis=0)
    pieces = jnp.concatenate([grads[:, :BLK], grads[:, BLK:]], axis=0).astype(bf16)
    back = jnp.concatenate([jnp.transpose(ds[b * BLK : (b + 1) * BLK]) for b in range(BPD)], axis=0).astype(bf16)
    for d in range(N_AX):
        out_ref[d, :n, :] = back
        out_ref[d, n:, :] = pieces[d * PIECE : (d + 1) * PIECE]


def adjoint_kernel(count_ref, rows_ref, cols_ref, adj_ref, got_ref, out_ref, acc_ref):
    def product(k):
        row = rows_ref[0, k]
        at = pl.multiple_of((row % BPD) * BLK, BLK)
        return dot(got_ref[row // BPD, pl.ds(at, BLK), :], adj_ref[k])

    slots_loop(count_ref, cols_ref, acc_ref, product)
    n = BPD * BLK
    grads = got_ref[0, n:, :].astype(f32)
    for d in range(1, N_AX):
        grads += got_ref[d, n:, :].astype(f32)
    grads = grads.astype(bf16)
    for d in range(N_AX):
        for b in range(BPD):
            out_ref[d, b * BLK : (b + 1) * BLK, :] = acc_ref[d * BPD + b].astype(bf16)
        out_ref[d, n:, :] = grads


def final_kernel(got_ref, dz_ref, ws_ref, out_ref, piece_ref):
    total = got_ref[0].astype(f32)
    for d in range(1, N_AX):
        total += got_ref[d].astype(f32)
    n = BPD * BLK
    adjoint = jnp.concatenate([jnp.transpose(total[b * BLK : (b + 1) * BLK]) for b in range(BPD)], axis=0)
    out_ref[...] = dot(dz_ref[...], ws_ref[...], ((1,), (1,))) + adjoint
    piece_ref[...] = total[n:].astype(bf16)


def call(kernel, out, scratch=(), flops=0, moved=0):
    return functools.partial(
        pl.pallas_call,
        kernel,
        out_shape=out,
        scratch_shapes=list(scratch),
        compiler_params=PARAMS,
        cost_estimate=pl.CostEstimate(flops=flops, bytes_accessed=moved, transcendentals=0),
    )


def exchange(x, axis):
    return lax.all_to_all(x, axis, 0, 0)


def local(features, cotangent, w_self, w_neigh, adj_blocks, block_rows, block_cols, block_count):
    adj = adj_blocks[0, 0]
    rows = block_rows[0]
    cols = block_cols[0]
    slots = adj.shape[0]
    n, width = features.shape
    product_flops = 2 * slots * BLK**3
    shape = jax.ShapeDtypeStruct
    sums_acc = pltpu.VMEM((STRIPE + 1, BLK, BLK), f32)

    column = exchange(jnp.broadcast_to(features[None], (N_AX, n, width)), "row")
    degree = call(
        degree_kernel,
        shape((N_AX, TAIL, BLK), bf16),
        [pltpu.VMEM((STRIPE + 1, 8, BLK), f32)],
        product_flops // 16,
        adj.size * 2,
    )(in_specs=[SMEM, SMEM, VMEM], out_specs=VMEM)(block_count, rows, adj)
    sums = call(
        forward_kernel, shape((N_AX, n + TAIL, BLK), bf16), [sums_acc], product_flops, adj.size * 4
    )(in_specs=[SMEM, SMEM, SMEM, VMEM, VMEM, VMEM], out_specs=VMEM)(
        block_count, rows, cols, adj, column.reshape(STRIPE, BLK, width), degree
    )
    sums = exchange(sums, "col")
    back, dz = call(
        dense_kernel, (shape((N_AX, n + PIECE, BLK), bf16), shape(cotangent.shape, bf16)), (), product_flops, adj.size
    )(in_specs=[VMEM] * 5, out_specs=(VMEM, VMEM))(sums, features, cotangent, w_self, w_neigh)
    back = exchange(back, "col")
    adjoint = call(
        adjoint_kernel, shape((N_AX, n + PIECE, BLK), bf16), [sums_acc], product_flops, adj.size * 4
    )(in_specs=[SMEM, SMEM, SMEM, VMEM, VMEM], out_specs=VMEM)(block_count, rows, cols, adj, back)
    adjoint = exchange(adjoint, "row")
    grad_features, piece = call(
        final_kernel, (shape((n, width), f32), shape((PIECE, BLK), bf16)), (), product_flops // 8, adj.size
    )(in_specs=[VMEM] * 3, out_specs=(VMEM, VMEM))(adjoint, dz, w_self)
    grads = exchange(jnp.broadcast_to(piece[None], (N_AX, PIECE, BLK)), "col")
    scale = (n * N_AX * N_AX) ** (-0.5)
    grads = grads.reshape(2, 2 * width, BLK).astype(f32) * scale
    grads = jnp.concatenate([grads[0], grads[1]], axis=1)
    return (grad_features, grads[:width], grads[width:])


def solution(mesh):
    placed = (
        P(("row", "col"), None),
        P(("row", "col"), None),
        P(),
        P(),
        P("row", "col", None, None, None),
        P("row", "col", None),
        P("row", "col", None),
        P("row", "col"),
    )
    return jax.shard_map(
        local,
        mesh=mesh,
        in_specs=placed,
        out_specs=(P(("row", "col"), None), P(), P()),
        check_vma=False,
    )
```

```python
import functools

import jax
import jax.numpy as jnp
from jax import lax
from jax.experimental import pallas as pl
from jax.experimental.pallas import tpu as pltpu
from jax.sharding import PartitionSpec as P

BLK = 128
N_AX = 16
BPD = 2
STRIPE = N_AX * BPD
UNROLL = 8
PIECE = 32
TAIL = 16
HALF = N_AX // 2
f32 = jnp.float32
bf16 = jnp.bfloat16

VMEM = pl.BlockSpec(memory_space=pltpu.VMEM)
SMEM = pl.BlockSpec(memory_space=pltpu.SMEM)
PARAMS = pltpu.CompilerParams(vmem_limit_bytes=24 * 1024 * 1024)


def dot(a, b, contract=((1,), (0,))):
    return lax.dot_general(a, b, (contract, ((), ())), preferred_element_type=f32)


def slots_loop(count_ref, index_ref, acc_ref, product):
    acc_ref[...] = jnp.zeros_like(acc_ref)
    count = count_ref[0, 0]

    def group(g, carry):
        base = g * UNROLL
        terms = [product(base + u) for u in range(UNROLL)]
        for u in range(UNROLL):
            k = base + u
            at = jnp.where(k < count, index_ref[0, k], STRIPE)
            acc_ref[at] += terms[u]
        return carry

    lax.fori_loop(0, (count + UNROLL - 1) // UNROLL, group, 0)


def wide(x):
    high = x.astype(bf16)
    return jnp.concatenate([high.astype(f32), x - high.astype(f32)], axis=0).astype(bf16)


def degree_kernel(count_ref, rows_ref, adj_ref, out_ref, acc_ref):
    ones = jnp.ones((8, BLK), bf16)
    slots_loop(count_ref, rows_ref, acc_ref, lambda k: dot(ones, adj_ref[k], ((1,), (1,))))
    for d in range(N_AX):
        parts = [acc_ref[d * BPD + b][0:1] for b in range(BPD)]
        both = jnp.concatenate(parts + parts + [jnp.zeros((TAIL - 2 * BPD, BLK), f32)], axis=0)
        high = both.astype(bf16)
        low = (both - high.astype(f32)).astype(bf16)
        at = lax.broadcasted_iota(jnp.int32, (TAIL, BLK), 0)
        out_ref[d] = jnp.where(at < BPD, high.astype(f32), low.astype(f32)).astype(bf16)


def forward_kernel(core_ref, count_ref, rows_ref, cols_ref, adj_ref, mine_ref, other_ref, deg_ref, out_ref, x_ref, acc_ref):
    core = core_ref[0]
    for p in range(HALF):
        x_ref[2 * p + core] = mine_ref[p]
        x_ref[2 * p + 1 - core] = other_ref[p]

    def product(k):
        col = cols_ref[0, k]
        at = pl.multiple_of((col % BPD) * BLK, BLK)
        return dot(adj_ref[k], x_ref[col // BPD, pl.ds(at, BLK), :])

    slots_loop(count_ref, rows_ref, acc_ref, product)
    for d in range(N_AX):
        for b in range(BPD):
            out_ref[d, b * BLK : (b + 1) * BLK, :] = acc_ref[d * BPD + b].astype(bf16)
        out_ref[d, BPD * BLK :, :] = deg_ref[d]


def dense_kernel(got_ref, x_ref, cot_ref, ws_ref, wn_ref, out_ref, dz_ref):
    total = got_ref[0].astype(f32)
    for d in range(1, N_AX):
        total += got_ref[d].astype(f32)
    n = BPD * BLK
    degree = total[n : n + BPD] + total[n + BPD : n + 2 * BPD]
    norm_lanes = lax.rsqrt(1.0 + degree)
    norm = jnp.concatenate(
        [jnp.transpose(jnp.broadcast_to(norm_lanes[b : b + 1], (BLK, BLK))) for b in range(BPD)], axis=0
    )
    agg = (total[:n] * norm).astype(bf16)
    x = x_ref[...]
    pre = dot(x, ws_ref[...]) + dot(agg, wn_ref[...])
    sig = jax.nn.sigmoid(pre)
    dz = (cot_ref[...].astype(f32) * (sig * (1.0 + pre * (1.0 - sig)))).astype(bf16)
    dz_ref[...] = dz
    ds = dot(dz, wn_ref[...], ((1,), (1,))) * norm
    grads = jnp.concatenate([dot(x, dz, ((0,), (0,))), dot(agg, dz, ((0,), (0,)))], axis=0)
    pieces = jnp.concatenate([grads[:, :BLK], grads[:, BLK:]], axis=0).astype(bf16)
    back = jnp.concatenate([jnp.transpose(ds[b * BLK : (b + 1) * BLK]) for b in range(BPD)], axis=0).astype(bf16)
    for d in range(N_AX):
        out_ref[d, :n, :] = back
        out_ref[d, n:, :] = pieces[d * PIECE : (d + 1) * PIECE]


def adjoint_kernel(core_ref, count_ref, rows_ref, cols_ref, adj_ref, got_ref, keep_ref, grads_ref, send_ref, acc_ref):
    def product(k):
        row = rows_ref[0, k]
        at = pl.multiple_of((row % BPD) * BLK, BLK)
        return dot(got_ref[row // BPD, pl.ds(at, BLK), :], adj_ref[k])

    slots_loop(count_ref, cols_ref, acc_ref, product)
    core = core_ref[0]
    n = BPD * BLK
    grads = got_ref[0, n:, :].astype(f32)
    for d in range(1, N_AX):
        grads += got_ref[d, n:, :].astype(f32)
    grads_ref[...] = grads
    for p in range(HALF):
        for b in range(BPD):
            keep_ref[p, b * BLK : (b + 1) * BLK, :] = acc_ref[(2 * p + core) * BPD + b]
            at = p * n + b * BLK
            send_ref[at : at + BLK, :] = acc_ref[(2 * p + 1 - core) * BPD + b].astype(bf16)
    send_ref[HALF * n :, :] = wide(grads)


def merge_kernel(keep_ref, grads_ref, got_ref, out_ref):
    n = BPD * BLK
    tail = got_ref[HALF * n :, :].astype(f32)
    grads = wide(grads_ref[...] + tail[:PIECE] + tail[PIECE:])
    for p in range(HALF):
        out_ref[p, :n, :] = (keep_ref[p] + got_ref[p * n : (p + 1) * n, :].astype(f32)).astype(bf16)
        out_ref[p, n:, :] = grads


def final_kernel(got_ref, dz_ref, ws_ref, out_ref, piece_ref):
    total = got_ref[0].astype(f32)
    for d in range(1, HALF):
        total += got_ref[d].astype(f32)
    n = BPD * BLK
    adjoint = jnp.concatenate([jnp.transpose(total[b * BLK : (b + 1) * BLK]) for b in range(BPD)], axis=0)
    out_ref[...] = dot(dz_ref[...], ws_ref[...], ((1,), (1,))) + adjoint
    piece_ref[...] = total[n : n + PIECE] + total[n + PIECE :]


def call(kernel, out, scratch=(), flops=0, moved=0):
    return functools.partial(
        pl.pallas_call,
        kernel,
        out_shape=out,
        scratch_shapes=list(scratch),
        compiler_params=PARAMS,
        cost_estimate=pl.CostEstimate(flops=flops, bytes_accessed=moved, transcendentals=0),
    )


def exchange(x, axis, groups=None):
    return lax.all_to_all(x, axis, 0, 0, axis_index_groups=groups)


SAME_CORE = [list(range(core, N_AX, 2)) for core in range(2)]
SWAP_CORE = [(i, i ^ 1) for i in range(N_AX)]


def local(features, cotangent, w_self, w_neigh, adj_blocks, block_rows, block_cols, block_count):
    adj = adj_blocks[0, 0]
    rows = block_rows[0]
    cols = block_cols[0]
    slots = adj.shape[0]
    n, width = features.shape
    product_flops = 2 * slots * BLK**3
    shape = jax.ShapeDtypeStruct
    sums_acc = pltpu.VMEM((STRIPE + 1, BLK, BLK), f32)
    core = (lax.axis_index("row") % 2).astype(jnp.int32).reshape(1)

    mine = exchange(jnp.broadcast_to(features[None], (HALF, n, width)), "row", SAME_CORE)
    other = lax.ppermute(mine, "row", SWAP_CORE)
    degree = call(
        degree_kernel,
        shape((N_AX, TAIL, BLK), bf16),
        [pltpu.VMEM((STRIPE + 1, 8, BLK), f32)],
        product_flops // 16,
        adj.size * 2,
    )(in_specs=[SMEM, SMEM, VMEM], out_specs=VMEM)(block_count, rows, adj)
    sums = call(
        forward_kernel,
        shape((N_AX, n + TAIL, BLK), bf16),
        [pltpu.VMEM((N_AX, n, width), bf16), sums_acc],
        product_flops,
        adj.size * 4,
    )(in_specs=[SMEM] * 4 + [VMEM] * 4, out_specs=VMEM)(
        core, block_count, rows, cols, adj, mine, other, degree
    )
    sums = exchange(sums, "col")
    back, dz = call(
        dense_kernel, (shape((N_AX, n + PIECE, BLK), bf16), shape(cotangent.shape, bf16)), (), product_flops, adj.size
    )(in_specs=[VMEM] * 5, out_specs=(VMEM, VMEM))(sums, features, cotangent, w_self, w_neigh)
    back = exchange(back, "col")
    keep, grads, send = call(
        adjoint_kernel,
        (
            shape((HALF, n, width), f32),
            shape((PIECE, BLK), f32),
            shape((HALF * n + 2 * PIECE, BLK), bf16),
        ),
        [sums_acc],
        product_flops,
        adj.size * 4,
    )(in_specs=[SMEM] * 4 + [VMEM] * 2, out_specs=(VMEM,) * 3)(core, block_count, rows, cols, adj, back)
    send = lax.ppermute(send, "row", SWAP_CORE)
    merged = call(merge_kernel, shape((HALF, n + 2 * PIECE, BLK), bf16), (), adj.size, adj.size)(
        in_specs=[VMEM] * 3, out_specs=VMEM
    )(keep, grads, send)
    merged = exchange(merged, "row", SAME_CORE)
    grad_features, piece = call(
        final_kernel, (shape((n, width), f32), shape((PIECE, BLK), f32)), (), product_flops // 8, adj.size
    )(in_specs=[VMEM] * 3, out_specs=(VMEM, VMEM))(merged, dz, w_self)
    grads = exchange(jnp.broadcast_to(piece[None], (N_AX, PIECE, BLK)), "col")
    scale = (n * N_AX * N_AX) ** (-0.5)
    grads = grads.reshape(2, 2 * width, BLK) * scale
    grads = jnp.concatenate([grads[0], grads[1]], axis=1)
    return (grad_features, grads[:width], grads[width:])


def solution(mesh):
    placed = (
        P(("row", "col"), None),
        P(("row", "col"), None),
        P(),
        P(),
        P("row", "col", None, None, None),
        P("row", "col", None),
        P("row", "col", None),
        P("row", "col"),
    )
    return jax.shard_map(
        local,
        mesh=mesh,
        in_specs=placed,
        out_specs=(P(("row", "col"), None), P(), P()),
        check_vma=False,
    )
```

```python
import functools

import jax
import jax.numpy as jnp
from jax import lax
from jax.experimental import pallas as pl
from jax.experimental.pallas import tpu as pltpu
from jax.sharding import PartitionSpec as P

BLK = 128
N_AX = 16
BPD = 2
STRIPE = N_AX * BPD
UNROLL = 8
PIECE = 32
TAIL = 16
HALF = N_AX // 2
Z = 8
NEAR = (0, 2, 6, 1, 7)
FAR = (4, 3, 5)
f32 = jnp.float32
bf16 = jnp.bfloat16

VMEM = pl.BlockSpec(memory_space=pltpu.VMEM)
SMEM = pl.BlockSpec(memory_space=pltpu.SMEM)
PARAMS = pltpu.CompilerParams(vmem_limit_bytes=24 * 1024 * 1024)


def dot(a, b, contract=((1,), (0,))):
    return lax.dot_general(a, b, (contract, ((), ())), preferred_element_type=f32)


def slots_loop(count_ref, index_ref, acc_ref, product):
    acc_ref[...] = jnp.zeros_like(acc_ref)
    count = count_ref[0, 0]

    def group(g, carry):
        base = g * UNROLL
        terms = [product(base + u) for u in range(UNROLL)]
        for u in range(UNROLL):
            k = base + u
            at = jnp.where(k < count, index_ref[0, k], STRIPE)
            acc_ref[at] += terms[u]
        return carry

    lax.fori_loop(0, (count + UNROLL - 1) // UNROLL, group, 0)


def wide(x):
    high = x.astype(bf16)
    return jnp.concatenate([high.astype(f32), x - high.astype(f32)], axis=0).astype(bf16)


def degree_kernel(count_ref, rows_ref, adj_ref, out_ref, acc_ref):
    ones = jnp.ones((8, BLK), bf16)
    slots_loop(count_ref, rows_ref, acc_ref, lambda k: dot(ones, adj_ref[k], ((1,), (1,))))
    for d in range(N_AX):
        parts = [acc_ref[d * BPD + b][0:1] for b in range(BPD)]
        both = jnp.concatenate(parts + parts + [jnp.zeros((TAIL - 2 * BPD, BLK), f32)], axis=0)
        high = both.astype(bf16)
        low = (both - high.astype(f32)).astype(bf16)
        at = lax.broadcasted_iota(jnp.int32, (TAIL, BLK), 0)
        out_ref[d] = jnp.where(at < BPD, high.astype(f32), low.astype(f32)).astype(bf16)


def forward_kernel(place_ref, count_ref, rows_ref, cols_ref, adj_ref, mine_ref, other_ref, deg_ref, out_ref, x_ref, acc_ref):
    core = place_ref[0]
    for p in range(HALF):
        x_ref[2 * p + core] = mine_ref[p]
        x_ref[2 * p + 1 - core] = other_ref[p]

    def product(k):
        col = cols_ref[0, k]
        at = pl.multiple_of((col % BPD) * BLK, BLK)
        return dot(adj_ref[k], x_ref[col // BPD, pl.ds(at, BLK), :])

    slots_loop(count_ref, rows_ref, acc_ref, product)
    for d in range(N_AX):
        for b in range(BPD):
            out_ref[d, b * BLK : (b + 1) * BLK, :] = acc_ref[d * BPD + b].astype(bf16)
        out_ref[d, BPD * BLK :, :] = deg_ref[d]


def narrow(parts):
    total = parts[0].astype(f32)
    for d in range(1, N_AX):
        total += parts[d].astype(f32)
    return total[:PIECE] + total[PIECE:]


def dense_kernel(got_ref, x_ref, cot_ref, ws_ref, wn_ref, back_ref, grads_ref, dz_ref):
    total = got_ref[0].astype(f32)
    for d in range(1, N_AX):
        total += got_ref[d].astype(f32)
    n = BPD * BLK
    degree = total[n : n + BPD] + total[n + BPD : n + 2 * BPD]
    norm_lanes = lax.rsqrt(1.0 + degree)
    norm = jnp.concatenate(
        [jnp.transpose(jnp.broadcast_to(norm_lanes[b : b + 1], (BLK, BLK))) for b in range(BPD)], axis=0
    )
    agg = (total[:n] * norm).astype(bf16)
    x = x_ref[...]
    pre = dot(x, ws_ref[...]) + dot(agg, wn_ref[...])
    sig = jax.nn.sigmoid(pre)
    dz = (cot_ref[...].astype(f32) * (sig * (1.0 + pre * (1.0 - sig)))).astype(bf16)
    dz_ref[...] = dz
    ds = dot(dz, wn_ref[...], ((1,), (1,))) * norm
    for b in range(BPD):
        back_ref[b * BLK : (b + 1) * BLK, :] = jnp.transpose(ds[b * BLK : (b + 1) * BLK]).astype(bf16)
    grads = jnp.concatenate([dot(x, dz, ((0,), (0,))), dot(agg, dz, ((0,), (0,)))], axis=0)
    pieces = jnp.concatenate([grads[:, :BLK], grads[:, BLK:]], axis=0)
    for d in range(N_AX):
        grads_ref[d] = wide(pieces[d * PIECE : (d + 1) * PIECE])


def stack_kernel(*refs):
    *parts, out_ref, again_ref = refs
    for j in range(out_ref.shape[0]):
        out_ref[j] = parts[j][...]
    again_ref[...] = parts[0][...]


def spread_kernel(got_ref, after_ref, out_ref):
    total = wide(narrow(got_ref))
    for d in range(N_AX):
        out_ref[d] = total


def piece_kernel(got_ref, out_ref):
    out_ref[...] = narrow(got_ref).astype(bf16)


def adjoint_kernel(
    place_ref, count_ref, rows_ref, cols_ref, adj_ref, near_ref, far_ref, near2_ref, far2_ref, after_ref, keep_ref, send_ref, x_ref, acc_ref
):
    z, yl = place_ref[1], place_ref[2]
    for mine, other, shifts in ((near_ref, near2_ref, NEAR), (far_ref, far2_ref, FAR)):
        for j, s in enumerate(shifts):
            at = 2 * ((z + Z - s) % Z)
            x_ref[at + yl] = mine[j]
            x_ref[at + 1 - yl] = other[j]

    def product(k):
        row = rows_ref[0, k]
        at = pl.multiple_of((row % BPD) * BLK, BLK)
        return dot(x_ref[row // BPD, pl.ds(at, BLK), :], adj_ref[k])

    slots_loop(count_ref, cols_ref, acc_ref, product)
    core = place_ref[0]
    n = BPD * BLK
    for p in range(HALF):
        for b in range(BPD):
            keep_ref[p, b * BLK : (b + 1) * BLK, :] = acc_ref[(2 * p + core) * BPD + b]
            send_ref[p, b * BLK : (b + 1) * BLK, :] = acc_ref[(2 * p + 1 - core) * BPD + b].astype(bf16)


def merge_kernel(place_ref, keep_ref, got_ref, piece_ref, piece2_ref, out_ref, both_ref):
    n = BPD * BLK
    core = place_ref[0]
    both_ref[core] = piece_ref[...]
    both_ref[1 - core] = piece2_ref[...]
    for p in range(HALF):
        out_ref[p, :n, :] = (keep_ref[p] + got_ref[p].astype(f32)).astype(bf16)
        for c in range(2):
            out_ref[p, n + c * PIECE : n + (c + 1) * PIECE, :] = both_ref[c]


def final_kernel(scale, got_ref, dz_ref, ws_ref, out_ref, self_ref, neigh_ref):
    n = BPD * BLK
    total = got_ref[0, :n, :].astype(f32)
    for d in range(1, HALF):
        total += got_ref[d, :n, :].astype(f32)
    adjoint = jnp.concatenate([jnp.transpose(total[b * BLK : (b + 1) * BLK]) for b in range(BPD)], axis=0)
    out_ref[...] = dot(dz_ref[...], ws_ref[...], ((1,), (1,))) + adjoint
    per = BLK // (2 * PIECE)
    for d in range(HALF):
        quarter, at = d // per, (d % per) * 2 * PIECE
        lanes = (quarter // 2) * BLK
        into = neigh_ref if quarter % 2 else self_ref
        into[at : at + 2 * PIECE, lanes : lanes + BLK] = got_ref[d, n:, :].astype(f32) * scale


def call(kernel, out, scratch=(), flops=0, moved=0):
    return functools.partial(
        pl.pallas_call,
        kernel,
        out_shape=out,
        scratch_shapes=list(scratch),
        compiler_params=PARAMS,
        cost_estimate=pl.CostEstimate(flops=flops, bytes_accessed=moved, transcendentals=0),
    )


def exchange(x, axis, groups=None):
    return lax.all_to_all(x, axis, 0, 0, axis_index_groups=groups)


SAME_CORE = [list(range(core, N_AX, 2)) for core in range(2)]
SWAP = [(i, i ^ 1) for i in range(N_AX)]


def z_shift(x, s):
    return lax.ppermute(x, "col", [(i, (i + 2 * s) % N_AX) for i in range(N_AX)])


def local(features, cotangent, w_self, w_neigh, adj_blocks, block_rows, block_cols, block_count):
    adj = adj_blocks[0, 0]
    rows = block_rows[0]
    cols = block_cols[0]
    slots = adj.shape[0]
    n, width = features.shape
    product_flops = 2 * slots * BLK**3
    shape = jax.ShapeDtypeStruct
    sums_acc = pltpu.VMEM((STRIPE + 1, BLK, BLK), f32)
    stripe = pltpu.VMEM((N_AX, n, width), bf16)
    row_at, col_at = lax.axis_index("row"), lax.axis_index("col")
    place = jnp.stack([row_at % 2, col_at // 2, col_at % 2]).astype(jnp.int32)

    mine = exchange(jnp.broadcast_to(features[None], (HALF, n, width)), "row", SAME_CORE)
    degree = call(
        degree_kernel,
        shape((N_AX, TAIL, BLK), bf16),
        [pltpu.VMEM((STRIPE + 1, 8, BLK), f32)],
        product_flops // 16,
        adj.size * 2,
    )(in_specs=[SMEM, SMEM, VMEM], out_specs=VMEM)(block_count, rows, adj)
    mine, degree = lax.optimization_barrier((mine, degree))
    other = lax.ppermute(mine, "row", SWAP)
    sums = call(
        forward_kernel, shape((N_AX, n + TAIL, BLK), bf16), [stripe, sums_acc], product_flops, adj.size * 4
    )(in_specs=[SMEM] * 4 + [VMEM] * 4, out_specs=VMEM)(
        place, block_count, rows, cols, adj, mine, other, degree
    )
    sums = exchange(sums, "col")
    back, grads, dz = call(
        dense_kernel,
        (shape((n, BLK), bf16), shape((N_AX, 2 * PIECE, BLK), bf16), shape(cotangent.shape, bf16)),
        (),
        product_flops,
        adj.size,
    )(in_specs=[VMEM] * 5, out_specs=(VMEM,) * 3)(sums, features, cotangent, w_self, w_neigh)

    grads = exchange(grads, "row")
    near = [back] + [z_shift(back, s) for s in NEAR[1:]]
    near, back = call(
        stack_kernel, (shape((len(NEAR), n, BLK), bf16), shape((n, BLK), bf16)), (), adj.size, adj.size
    )(in_specs=[VMEM] * len(NEAR), out_specs=(VMEM, VMEM))(*near)
    far = jnp.stack([z_shift(back, s) for s in FAR])
    near2 = lax.ppermute(near, "col", SWAP)
    far2 = lax.ppermute(far, "col", SWAP)
    grads = call(spread_kernel, shape(grads.shape, bf16), (), adj.size, adj.size)(
        in_specs=[VMEM, pl.BlockSpec(memory_space=pl.ANY)], out_specs=VMEM
    )(grads, near)
    grads = exchange(grads, "col")
    piece = call(piece_kernel, shape((PIECE, BLK), bf16), (), adj.size, adj.size)(in_specs=[VMEM], out_specs=VMEM)(grads)
    piece2 = lax.ppermute(piece, "row", SWAP)

    keep, send = call(
        adjoint_kernel,
        (shape((HALF, n, width), f32), shape((HALF, n, width), bf16)),
        [stripe, sums_acc],
        product_flops,
        adj.size * 4,
    )(in_specs=[SMEM] * 4 + [VMEM] * 5 + [pl.BlockSpec(memory_space=pl.ANY)], out_specs=(VMEM,) * 2)(
        place, block_count, rows, cols, adj, near, far, near2, far2, piece
    )
    send = lax.ppermute(send, "row", SWAP)
    merged = call(
        merge_kernel,
        shape((HALF, n + 2 * PIECE, BLK), bf16),
        [pltpu.VMEM((2, PIECE, BLK), bf16)],
        adj.size,
        adj.size,
    )(in_specs=[SMEM] + [VMEM] * 4, out_specs=VMEM)(place, keep, send, piece, piece2)
    merged = exchange(merged, "row", SAME_CORE)
    scale = (n * N_AX * N_AX) ** (-0.5)
    return call(
        functools.partial(final_kernel, scale),
        (shape((n, width), f32), shape(w_self.shape, f32), shape(w_neigh.shape, f32)),
        (),
        product_flops // 8,
        adj.size,
    )(in_specs=[VMEM] * 3, out_specs=(VMEM,) * 3)(merged, dz, w_self)


def solution(mesh):
    placed = (
        P(("row", "col"), None),
        P(("row", "col"), None),
        P(),
        P(),
        P("row", "col", None, None, None),
        P("row", "col", None),
        P("row", "col", None),
        P("row", "col"),
    )
    return jax.shard_map(
        local,
        mesh=mesh,
        in_specs=placed,
        out_specs=(P(("row", "col"), None), P(), P()),
        check_vma=False,
    )
```

```python
import functools

import jax
import jax.numpy as jnp
from jax import lax
from jax.experimental import pallas as pl
from jax.experimental.pallas import tpu as pltpu
from jax.sharding import PartitionSpec as P

BLK = 128
N_AX = 16
BPD = 2
STRIPE = N_AX * BPD
UNROLL = 8
PIECE = 32
TAIL = 16
HALF = N_AX // 2
Z = 8
NEAR = (0, 2, 6, 1, 7)
FAR = (4, 3, 5)
EVEN = (0, 4, 2, 6)
ODD = (1, 5, 7, 3)
f32 = jnp.float32
bf16 = jnp.bfloat16

VMEM = pl.BlockSpec(memory_space=pltpu.VMEM)
ANY = pl.BlockSpec(memory_space=pl.ANY)
SMEM = pl.BlockSpec(memory_space=pltpu.SMEM)
PARAMS = pltpu.CompilerParams(vmem_limit_bytes=24 * 1024 * 1024)


def dot(a, b, contract=((1,), (0,))):
    return lax.dot_general(a, b, (contract, ((), ())), preferred_element_type=f32)


def slots_loop(count_ref, index_ref, acc_ref, product):
    acc_ref[...] = jnp.zeros_like(acc_ref)
    count = count_ref[0, 0]

    def group(g, carry):
        base = g * UNROLL
        terms = [product(base + u) for u in range(UNROLL)]
        for u in range(UNROLL):
            k = base + u
            at = jnp.where(k < count, index_ref[0, k], STRIPE)
            acc_ref[at] += terms[u]
        return carry

    lax.fori_loop(0, (count + UNROLL - 1) // UNROLL, group, 0)


def wide(x):
    high = x.astype(bf16)
    return jnp.concatenate([high.astype(f32), x - high.astype(f32)], axis=0).astype(bf16)


def degree_kernel(count_ref, rows_ref, adj_ref, out_ref, acc_ref):
    ones = jnp.ones((8, BLK), bf16)
    slots_loop(count_ref, rows_ref, acc_ref, lambda k: dot(ones, adj_ref[k], ((1,), (1,))))
    for d in range(N_AX):
        parts = [acc_ref[d * BPD + b][0:1] for b in range(BPD)]
        out_ref[d] = jnp.concatenate(parts + [jnp.zeros((8 - BPD, BLK), f32)], axis=0)


def tail_of(degree):
    low = degree - degree.astype(bf16).astype(f32)
    parts = [degree[:BPD], low[:BPD], jnp.zeros((TAIL - 2 * BPD, BLK), f32)]
    return jnp.concatenate(parts, axis=0).astype(bf16)


def degree_of(tail):
    tail = tail.astype(f32)
    return jnp.concatenate([tail[:BPD] + tail[BPD : 2 * BPD], jnp.zeros((8 - BPD, BLK), f32)], axis=0)


def forward_kernel(
    place_ref, count_ref, rows_ref, cols_ref, adj_ref, mine_ref, other_ref, deg_ref,
    near_ref, far_ref, near_deg_ref, far_deg_ref, near_send_ref, far_send_ref, x_ref, acc_ref,
):
    core, z, yl = place_ref[0], place_ref[1], place_ref[2]
    for p in range(HALF):
        x_ref[2 * p + core] = mine_ref[p]
        x_ref[2 * p + 1 - core] = other_ref[p]

    def product(k):
        col = cols_ref[0, k]
        at = pl.multiple_of((col % BPD) * BLK, BLK)
        return dot(adj_ref[k], x_ref[col // BPD, pl.ds(at, BLK), :])

    slots_loop(count_ref, rows_ref, acc_ref, product)
    n = BPD * BLK
    for keep, degree, send, shifts in (
        (far_ref, far_deg_ref, far_send_ref, FAR),
        (near_ref, near_deg_ref, near_send_ref, NEAR),
    ):
        for j, s in enumerate(shifts):
            at = 2 * ((z + s) % Z)
            here, there = at + yl, at + 1 - yl
            for b in range(BPD):
                keep[j, b * BLK : (b + 1) * BLK, :] = acc_ref[here * BPD + b]
                send[j, b * BLK : (b + 1) * BLK, :] = acc_ref[there * BPD + b].astype(bf16)
            degree[j] = deg_ref[here]
            send[j, n:, :] = tail_of(deg_ref[there])


def gate_kernel(x_ref, after_ref, out_ref):
    pass


def pair_kernel(keep_ref, deg_ref, got_ref, *out_refs):
    n = BPD * BLK
    first = len(out_refs) - keep_ref.shape[0]
    if first:
        own_ref, own_deg_ref, *out_refs = out_refs
        own_ref[...] = keep_ref[0] + got_ref[0, :n, :].astype(f32)
        own_deg_ref[...] = deg_ref[0] + degree_of(got_ref[0, n:, :])
    for j, out_ref in enumerate(out_refs, first):
        out_ref[:n, :] = (keep_ref[j] + got_ref[j, :n, :].astype(f32)).astype(bf16)
        out_ref[n:, :] = tail_of(deg_ref[j] + degree_of(got_ref[j, n:, :]))


def narrow(parts):
    total = parts[0].astype(f32)
    for d in range(1, N_AX):
        total += parts[d].astype(f32)
    return total[:PIECE] + total[PIECE:]


def dense_kernel(own_ref, own_deg_ref, *refs):
    *got_refs, x_ref, cot_ref, ws_ref, wn_ref, back_ref, grads_ref, dz_ref = refs
    n = BPD * BLK
    total = own_ref[...]
    degree = own_deg_ref[...]
    for got_ref in got_refs:
        total += got_ref[:n, :].astype(f32)
        degree += degree_of(got_ref[n:, :])
    norm_lanes = lax.rsqrt(1.0 + degree)
    norm = jnp.concatenate(
        [jnp.transpose(jnp.broadcast_to(norm_lanes[b : b + 1], (BLK, BLK))) for b in range(BPD)], axis=0
    )
    agg = (total * norm).astype(bf16)
    x = x_ref[...]
    pre = dot(x, ws_ref[...]) + dot(agg, wn_ref[...])
    sig = jax.nn.sigmoid(pre)
    dz = (cot_ref[...].astype(f32) * (sig * (1.0 + pre * (1.0 - sig)))).astype(bf16)
    dz_ref[...] = dz
    ds = dot(dz, wn_ref[...], ((1,), (1,))) * norm
    for b in range(BPD):
        back_ref[b * BLK : (b + 1) * BLK, :] = jnp.transpose(ds[b * BLK : (b + 1) * BLK]).astype(bf16)
    grads = jnp.concatenate([dot(x, dz, ((0,), (0,))), dot(agg, dz, ((0,), (0,)))], axis=0)
    pieces = jnp.concatenate([grads[:, :BLK], grads[:, BLK:]], axis=0)
    for d in range(N_AX):
        grads_ref[d] = wide(pieces[d * PIECE : (d + 1) * PIECE])


def stack_kernel(*refs):
    *parts, out_ref = refs
    for j, part in enumerate(parts):
        out_ref[j] = part[...]


def spread_kernel(got_ref, after_ref, after2_ref, out_ref):
    total = wide(narrow(got_ref))
    for d in range(N_AX):
        out_ref[d] = total


def piece_kernel(got_ref, out_ref):
    out_ref[...] = narrow(got_ref).astype(bf16)


def adjoint_kernel(
    place_ref, count_ref, rows_ref, cols_ref, adj_ref, even_ref, odd_ref, even2_ref, odd2_ref, after_ref, keep_ref, send_ref, x_ref, acc_ref
):
    z, yl = place_ref[1], place_ref[2]
    for mine, other, shifts in ((even_ref, even2_ref, EVEN), (odd_ref, odd2_ref, ODD)):
        for j, s in enumerate(shifts):
            at = 2 * ((z + Z - s) % Z)
            x_ref[at + yl] = mine[j]
            x_ref[at + 1 - yl] = other[j]

    def product(k):
        row = rows_ref[0, k]
        at = pl.multiple_of((row % BPD) * BLK, BLK)
        return dot(x_ref[row // BPD, pl.ds(at, BLK), :], adj_ref[k])

    slots_loop(count_ref, cols_ref, acc_ref, product)
    core = place_ref[0]
    n = BPD * BLK
    for p in range(HALF):
        for b in range(BPD):
            keep_ref[p, b * BLK : (b + 1) * BLK, :] = acc_ref[(2 * p + core) * BPD + b]
            send_ref[p, b * BLK : (b + 1) * BLK, :] = acc_ref[(2 * p + 1 - core) * BPD + b].astype(bf16)


def merge_kernel(place_ref, keep_ref, got_ref, piece_ref, piece2_ref, out_ref, both_ref):
    n = BPD * BLK
    core = place_ref[0]
    both_ref[core] = piece_ref[...]
    both_ref[1 - core] = piece2_ref[...]
    for p in range(HALF):
        out_ref[p, :n, :] = (keep_ref[p] + got_ref[p].astype(f32)).astype(bf16)
        for c in range(2):
            out_ref[p, n + c * PIECE : n + (c + 1) * PIECE, :] = both_ref[c]


def final_kernel(scale, got_ref, dz_ref, ws_ref, out_ref, self_ref, neigh_ref):
    n = BPD * BLK
    total = got_ref[0, :n, :].astype(f32)
    for d in range(1, HALF):
        total += got_ref[d, :n, :].astype(f32)
    adjoint = jnp.concatenate([jnp.transpose(total[b * BLK : (b + 1) * BLK]) for b in range(BPD)], axis=0)
    out_ref[...] = dot(dz_ref[...], ws_ref[...], ((1,), (1,))) + adjoint
    per = BLK // (2 * PIECE)
    for d in range(HALF):
        quarter, at = d // per, (d % per) * 2 * PIECE
        lanes = (quarter // 2) * BLK
        into = neigh_ref if quarter % 2 else self_ref
        into[at : at + 2 * PIECE, lanes : lanes + BLK] = got_ref[d, n:, :].astype(f32) * scale


def call(kernel, out, scratch=(), flops=0, moved=0):
    return functools.partial(
        pl.pallas_call,
        kernel,
        out_shape=out,
        scratch_shapes=list(scratch),
        compiler_params=PARAMS,
        cost_estimate=pl.CostEstimate(flops=flops, bytes_accessed=moved, transcendentals=0),
    )


def exchange(x, axis, groups=None):
    return lax.all_to_all(x, axis, 0, 0, axis_index_groups=groups)


SAME_CORE = [list(range(core, N_AX, 2)) for core in range(2)]
SWAP = [(i, i ^ 1) for i in range(N_AX)]


def z_shift(x, s):
    return lax.ppermute(x, "col", [(i, (i + 2 * s) % N_AX) for i in range(N_AX)])


def local(features, cotangent, w_self, w_neigh, adj_blocks, block_rows, block_cols, block_count):
    adj = adj_blocks[0, 0]
    rows = block_rows[0]
    cols = block_cols[0]
    slots = adj.shape[0]
    n, width = features.shape
    product_flops = 2 * slots * BLK**3
    shape = jax.ShapeDtypeStruct
    sums_acc = pltpu.VMEM((STRIPE + 1, BLK, BLK), f32)
    stripe = pltpu.VMEM((N_AX, n, width), bf16)
    row_at, col_at = lax.axis_index("row"), lax.axis_index("col")
    place = jnp.stack([row_at % 2, col_at // 2, col_at % 2]).astype(jnp.int32)

    mine = exchange(jnp.broadcast_to(features[None], (HALF, n, width)), "row", SAME_CORE)
    degree = call(
        degree_kernel,
        shape((N_AX, 8, BLK), f32),
        [pltpu.VMEM((STRIPE + 1, 8, BLK), f32)],
        product_flops // 16,
        adj.size * 2,
    )(in_specs=[SMEM, SMEM, VMEM], out_specs=VMEM)(block_count, rows, adj)
    mine, degree = lax.optimization_barrier((mine, degree))
    other = lax.ppermute(mine, "row", SWAP)
    near, far = len(NEAR), len(FAR)
    near_keep, far_keep, near_deg, far_deg, near_send, far_send = call(
        forward_kernel,
        (
            shape((near, n, BLK), f32),
            shape((far, n, BLK), f32),
            shape((near, 8, BLK), f32),
            shape((far, 8, BLK), f32),
            shape((near, n + TAIL, BLK), bf16),
            shape((far, n + TAIL, BLK), bf16),
        ),
        [stripe, sums_acc],
        product_flops,
        adj.size * 4,
    )(in_specs=[SMEM] * 4 + [VMEM] * 4, out_specs=(VMEM,) * 6)(
        place, block_count, rows, cols, adj, mine, other, degree
    )
    far_got = lax.ppermute(far_send, "col", SWAP)
    near_send = call(gate_kernel, shape(near_send.shape, bf16))(
        in_specs=[ANY, ANY], out_specs=ANY, input_output_aliases={0: 0}
    )(near_send, far_got)
    near_got = lax.ppermute(near_send, "col", SWAP)
    block = shape((n + TAIL, BLK), bf16)
    far_out = call(pair_kernel, (block,) * far, (), adj.size, adj.size)(
        in_specs=[VMEM] * 3, out_specs=(VMEM,) * far
    )(far_keep, far_deg, far_got)
    own, own_deg, *near_out = call(
        pair_kernel, (shape((n, BLK), f32), shape((8, BLK), f32)) + (block,) * (near - 1), (), adj.size, adj.size
    )(in_specs=[VMEM] * 3, out_specs=(VMEM,) * (near + 1))(near_keep, near_deg, near_got)
    sums = [z_shift(x, s) for x, s in zip(far_out, FAR)] + [z_shift(x, s) for x, s in zip(near_out, NEAR[1:])]
    back, grads, dz = call(
        dense_kernel,
        (shape((n, BLK), bf16), shape((N_AX, 2 * PIECE, BLK), bf16), shape(cotangent.shape, bf16)),
        (),
        product_flops,
        adj.size,
    )(in_specs=[VMEM] * (6 + len(sums)), out_specs=(VMEM,) * 3)(own, own_deg, *sums, features, cotangent, w_self, w_neigh)

    grads = exchange(grads, "row")
    opposite = z_shift(back, 4)
    even = [back, opposite, z_shift(back, 2), z_shift(back, 6)]
    two = jnp.stack([back, opposite])
    even = call(stack_kernel, shape((4, n, BLK), bf16), (), adj.size, adj.size)(
        in_specs=[VMEM] * 4, out_specs=VMEM
    )(*even)
    even2 = lax.ppermute(even, "col", SWAP)
    odd = [z_shift(two, 1), z_shift(two, 7)]
    odd = call(stack_kernel, shape((2, 2, n, BLK), bf16), (), adj.size, adj.size)(
        in_specs=[VMEM] * 2, out_specs=VMEM
    )(*odd).reshape(4, n, BLK)
    odd_at = odd
    odd = call(gate_kernel, shape(odd.shape, bf16))(
        in_specs=[ANY, ANY], out_specs=ANY, input_output_aliases={0: 0}
    )(odd, even2)
    odd2 = lax.ppermute(odd, "col", SWAP)
    grads = call(spread_kernel, shape(grads.shape, bf16), (), adj.size, adj.size)(
        in_specs=[VMEM, ANY, ANY], out_specs=VMEM
    )(grads, even, odd_at)
    grads = exchange(grads, "col")
    piece = call(piece_kernel, shape((PIECE, BLK), bf16), (), adj.size, adj.size)(in_specs=[VMEM], out_specs=VMEM)(grads)
    piece2 = lax.ppermute(piece, "row", SWAP)

    keep, send = call(
        adjoint_kernel,
        (shape((HALF, n, width), f32), shape((HALF, n, width), bf16)),
        [stripe, sums_acc],
        product_flops,
        adj.size * 4,
    )(in_specs=[SMEM] * 4 + [VMEM] * 5 + [ANY], out_specs=(VMEM,) * 2)(
        place, block_count, rows, cols, adj, even, odd, even2, odd2, piece
    )
    send = lax.ppermute(send, "row", SWAP)
    merged = call(
        merge_kernel,
        shape((HALF, n + 2 * PIECE, BLK), bf16),
        [pltpu.VMEM((2, PIECE, BLK), bf16)],
        adj.size,
        adj.size,
    )(in_specs=[SMEM] + [VMEM] * 4, out_specs=VMEM)(place, keep, send, piece, piece2)
    merged = exchange(merged, "row", SAME_CORE)
    scale = (n * N_AX * N_AX) ** (-0.5)
    return call(
        functools.partial(final_kernel, scale),
        (shape((n, width), f32), shape(w_self.shape, f32), shape(w_neigh.shape, f32)),
        (),
        product_flops // 8,
        adj.size,
    )(in_specs=[VMEM] * 3, out_specs=(VMEM,) * 3)(merged, dz, w_self)


def solution(mesh):
    placed = (
        P(("row", "col"), None),
        P(("row", "col"), None),
        P(),
        P(),
        P("row", "col", None, None, None),
        P("row", "col", None),
        P("row", "col", None),
        P("row", "col"),
    )
    return jax.shard_map(
        local,
        mesh=mesh,
        in_specs=placed,
        out_specs=(P(("row", "col"), None), P(), P()),
        check_vma=False,
    )
```

```python
import functools

import jax
import jax.numpy as jnp
from jax import lax
from jax.experimental import pallas as pl
from jax.experimental.pallas import tpu as pltpu
from jax.sharding import PartitionSpec as P

BLK = 128
N_AX = 16
BPD = 2
STRIPE = N_AX * BPD
UNROLL = 16
PIECE = 32
TAIL = 16
HALF = N_AX // 2
Z = 8
NEAR = (0, 2, 6, 1, 7)
FAR = (4, 3, 5)
SHIFTS = (0, 4, 1, 5, 7, 3, 2, 6)
f32 = jnp.float32
bf16 = jnp.bfloat16

VMEM = pl.BlockSpec(memory_space=pltpu.VMEM)
ANY = pl.BlockSpec(memory_space=pl.ANY)
SMEM = pl.BlockSpec(memory_space=pltpu.SMEM)
PARAMS = pltpu.CompilerParams(vmem_limit_bytes=24 * 1024 * 1024)


def dot(a, b, contract=((1,), (0,))):
    return lax.dot_general(a, b, (contract, ((), ())), preferred_element_type=f32)


def slots_loop(count_ref, index_ref, acc_ref, product):
    acc_ref[...] = jnp.zeros_like(acc_ref)
    count = count_ref[0, 0]

    def group(g, carry):
        base = g * UNROLL
        terms = [product(base + u) for u in range(UNROLL)]
        for u in range(UNROLL):
            k = base + u
            at = jnp.where(k < count, index_ref[0, k], STRIPE)
            acc_ref[at] += terms[u]
        return carry

    lax.fori_loop(0, (count + UNROLL - 1) // UNROLL, group, 0)


def wide(x):
    high = x.astype(bf16)
    return jnp.concatenate([high.astype(f32), x - high.astype(f32)], axis=0).astype(bf16)


def degree_kernel(count_ref, rows_ref, adj_ref, out_ref, acc_ref):
    ones = jnp.ones((8, BLK), bf16)
    slots_loop(count_ref, rows_ref, acc_ref, lambda k: dot(ones, adj_ref[k], ((1,), (1,))))
    for d in range(N_AX):
        parts = [acc_ref[d * BPD + b][0:1] for b in range(BPD)]
        out_ref[d] = jnp.concatenate(parts + [jnp.zeros((8 - BPD, BLK), f32)], axis=0)


def tail_of(degree):
    low = degree - degree.astype(bf16).astype(f32)
    parts = [degree[:BPD], low[:BPD], jnp.zeros((TAIL - 2 * BPD, BLK), f32)]
    return jnp.concatenate(parts, axis=0).astype(bf16)


def degree_of(tail):
    tail = tail.astype(f32)
    return jnp.concatenate([tail[:BPD] + tail[BPD : 2 * BPD], jnp.zeros((8 - BPD, BLK), f32)], axis=0)


def forward_kernel(
    place_ref, count_ref, rows_ref, cols_ref, adj_ref, mine_ref, other_ref, deg_ref,
    near_ref, far_ref, near_deg_ref, far_deg_ref, near_send_ref, far_send_ref, x_ref, acc_ref,
):
    core, z, yl = place_ref[0], place_ref[1], place_ref[2]
    for p in range(HALF):
        x_ref[2 * p + core] = mine_ref[p]
        x_ref[2 * p + 1 - core] = other_ref[p]

    def product(k):
        col = cols_ref[0, k]
        at = pl.multiple_of((col % BPD) * BLK, BLK)
        return dot(adj_ref[k], x_ref[col // BPD, pl.ds(at, BLK), :])

    slots_loop(count_ref, rows_ref, acc_ref, product)
    n = BPD * BLK
    for keep, degree, send, shifts in (
        (far_ref, far_deg_ref, far_send_ref, FAR),
        (near_ref, near_deg_ref, near_send_ref, NEAR),
    ):
        for j, s in enumerate(shifts):
            at = 2 * ((z + s) % Z)
            here, there = at + yl, at + 1 - yl
            for b in range(BPD):
                keep[j, b * BLK : (b + 1) * BLK, :] = acc_ref[here * BPD + b]
                send[j, b * BLK : (b + 1) * BLK, :] = acc_ref[there * BPD + b].astype(bf16)
            degree[j] = deg_ref[here]
            send[j, n:, :] = tail_of(deg_ref[there])


def gate_kernel(x_ref, after_ref, out_ref):
    pass


def pair_kernel(keep_ref, deg_ref, got_ref, *out_refs):
    n = BPD * BLK
    first = len(out_refs) - keep_ref.shape[0]
    if first:
        own_ref, own_deg_ref, *out_refs = out_refs
        own_ref[...] = keep_ref[0] + got_ref[0, :n, :].astype(f32)
        own_deg_ref[...] = deg_ref[0] + degree_of(got_ref[0, n:, :])
    for j, out_ref in enumerate(out_refs, first):
        out_ref[:n, :] = (keep_ref[j] + got_ref[j, :n, :].astype(f32)).astype(bf16)
        out_ref[n:, :] = tail_of(deg_ref[j] + degree_of(got_ref[j, n:, :]))


def narrow(parts):
    total = parts[0].astype(f32)
    for d in range(1, N_AX):
        total += parts[d].astype(f32)
    return total[:PIECE] + total[PIECE:]


def dense_kernel(own_ref, own_deg_ref, *refs):
    *got_refs, x_ref, cot_ref, ws_ref, wn_ref, back_ref, grads_ref, dz_ref = refs
    n = BPD * BLK
    total = own_ref[...]
    degree = own_deg_ref[...]
    for got_ref in got_refs:
        total += got_ref[:n, :].astype(f32)
        degree += degree_of(got_ref[n:, :])
    norm_lanes = lax.rsqrt(1.0 + degree)
    norm = jnp.concatenate(
        [jnp.transpose(jnp.broadcast_to(norm_lanes[b : b + 1], (BLK, BLK))) for b in range(BPD)], axis=0
    )
    agg = (total * norm).astype(bf16)
    x = x_ref[...]
    pre = dot(x, ws_ref[...]) + dot(agg, wn_ref[...])
    sig = jax.nn.sigmoid(pre)
    dz = (cot_ref[...].astype(f32) * (sig * (1.0 + pre * (1.0 - sig)))).astype(bf16)
    dz_ref[...] = dz
    ds = dot(dz, wn_ref[...], ((1,), (1,))) * norm
    for b in range(BPD):
        back_ref[b * BLK : (b + 1) * BLK, :] = jnp.transpose(ds[b * BLK : (b + 1) * BLK]).astype(bf16)
    grads = jnp.concatenate([dot(x, dz, ((0,), (0,))), dot(agg, dz, ((0,), (0,)))], axis=0)
    pieces = jnp.concatenate([grads[:, :BLK], grads[:, BLK:]], axis=0)
    for d in range(N_AX):
        grads_ref[d] = wide(pieces[d * PIECE : (d + 1) * PIECE])


def stack_kernel(*refs):
    *parts, out_ref = refs
    at = 0
    for part in parts:
        count = part.shape[0] if len(part.shape) == 3 else 1
        out_ref[at : at + count] = part[...].reshape(count, *out_ref.shape[1:])
        at += count


def spread_kernel(got_ref, after_ref, out_ref):
    total = wide(narrow(got_ref))
    for d in range(N_AX):
        out_ref[d] = total


def piece_kernel(got_ref, out_ref):
    out_ref[...] = narrow(got_ref).astype(bf16)


def adjoint_kernel(
    place_ref, count_ref, rows_ref, cols_ref, adj_ref, mine_ref, other_ref, after_ref, keep_ref, send_ref, x_ref, acc_ref
):
    z, yl = place_ref[1], place_ref[2]
    for j, s in enumerate(SHIFTS):
        at = 2 * ((z + Z - s) % Z)
        x_ref[at + yl] = mine_ref[j]
        x_ref[at + 1 - yl] = other_ref[j]

    def product(k):
        row = rows_ref[0, k]
        at = pl.multiple_of((row % BPD) * BLK, BLK)
        return dot(x_ref[row // BPD, pl.ds(at, BLK), :], adj_ref[k])

    slots_loop(count_ref, cols_ref, acc_ref, product)
    core = place_ref[0]
    n = BPD * BLK
    for p in range(HALF):
        for b in range(BPD):
            keep_ref[p, b * BLK : (b + 1) * BLK, :] = acc_ref[(2 * p + core) * BPD + b]
            send_ref[p, b * BLK : (b + 1) * BLK, :] = acc_ref[(2 * p + 1 - core) * BPD + b].astype(bf16)


def merge_kernel(place_ref, keep_ref, got_ref, piece_ref, piece2_ref, out_ref, both_ref):
    n = BPD * BLK
    core = place_ref[0]
    both_ref[core] = piece_ref[...]
    both_ref[1 - core] = piece2_ref[...]
    for p in range(HALF):
        out_ref[p, :n, :] = (keep_ref[p] + got_ref[p].astype(f32)).astype(bf16)
        for c in range(2):
            out_ref[p, n + c * PIECE : n + (c + 1) * PIECE, :] = both_ref[c]


def final_kernel(scale, got_ref, dz_ref, ws_ref, out_ref, self_ref, neigh_ref):
    n = BPD * BLK
    total = got_ref[0, :n, :].astype(f32)
    for d in range(1, HALF):
        total += got_ref[d, :n, :].astype(f32)
    adjoint = jnp.concatenate([jnp.transpose(total[b * BLK : (b + 1) * BLK]) for b in range(BPD)], axis=0)
    out_ref[...] = dot(dz_ref[...], ws_ref[...], ((1,), (1,))) + adjoint
    per = BLK // (2 * PIECE)
    for d in range(HALF):
        quarter, at = d // per, (d % per) * 2 * PIECE
        lanes = (quarter // 2) * BLK
        into = neigh_ref if quarter % 2 else self_ref
        into[at : at + 2 * PIECE, lanes : lanes + BLK] = got_ref[d, n:, :].astype(f32) * scale


def call(kernel, out, scratch=(), flops=0, moved=0):
    return functools.partial(
        pl.pallas_call,
        kernel,
        out_shape=out,
        scratch_shapes=list(scratch),
        compiler_params=PARAMS,
        cost_estimate=pl.CostEstimate(flops=flops, bytes_accessed=moved, transcendentals=0),
    )


def exchange(x, axis, groups=None):
    return lax.all_to_all(x, axis, 0, 0, axis_index_groups=groups)


SAME_CORE = [list(range(core, N_AX, 2)) for core in range(2)]
SWAP = [(i, i ^ 1) for i in range(N_AX)]


def z_shift(x, s):
    return lax.ppermute(x, "col", [(i, (i + 2 * s) % N_AX) for i in range(N_AX)])


def local(features, cotangent, w_self, w_neigh, adj_blocks, block_rows, block_cols, block_count):
    adj = adj_blocks[0, 0]
    rows = block_rows[0]
    cols = block_cols[0]
    slots = adj.shape[0]
    n, width = features.shape
    product_flops = 2 * slots * BLK**3
    shape = jax.ShapeDtypeStruct
    sums_acc = pltpu.VMEM((STRIPE + 1, BLK, BLK), f32)
    stripe = pltpu.VMEM((N_AX, n, width), bf16)
    row_at, col_at = lax.axis_index("row"), lax.axis_index("col")
    place = jnp.stack([row_at % 2, col_at // 2, col_at % 2]).astype(jnp.int32)

    mine = exchange(jnp.broadcast_to(features[None], (HALF, n, width)), "row", SAME_CORE)
    degree = call(
        degree_kernel,
        shape((N_AX, 8, BLK), f32),
        [pltpu.VMEM((STRIPE + 1, 8, BLK), f32)],
        product_flops // 16,
        adj.size * 2,
    )(in_specs=[SMEM, SMEM, VMEM], out_specs=VMEM)(block_count, rows, adj)
    mine, degree = lax.optimization_barrier((mine, degree))
    other = lax.ppermute(mine, "row", SWAP)
    near, far = len(NEAR), len(FAR)
    near_keep, far_keep, near_deg, far_deg, near_send, far_send = call(
        forward_kernel,
        (
            shape((near, n, BLK), f32),
            shape((far, n, BLK), f32),
            shape((near, 8, BLK), f32),
            shape((far, 8, BLK), f32),
            shape((near, n + TAIL, BLK), bf16),
            shape((far, n + TAIL, BLK), bf16),
        ),
        [stripe, sums_acc],
        product_flops,
        adj.size * 4,
    )(in_specs=[SMEM] * 4 + [VMEM] * 4, out_specs=(VMEM,) * 6)(
        place, block_count, rows, cols, adj, mine, other, degree
    )
    far_got = lax.ppermute(far_send, "col", SWAP)
    near_send = call(gate_kernel, shape(near_send.shape, bf16))(
        in_specs=[ANY, ANY], out_specs=ANY, input_output_aliases={0: 0}
    )(near_send, far_got)
    near_got = lax.ppermute(near_send, "col", SWAP)
    block = shape((n + TAIL, BLK), bf16)
    far_out = call(pair_kernel, (block,) * far, (), adj.size, adj.size)(
        in_specs=[VMEM] * 3, out_specs=(VMEM,) * far
    )(far_keep, far_deg, far_got)
    own, own_deg, *near_out = call(
        pair_kernel, (shape((n, BLK), f32), shape((8, BLK), f32)) + (block,) * (near - 1), (), adj.size, adj.size
    )(in_specs=[VMEM] * 3, out_specs=(VMEM,) * (near + 1))(near_keep, near_deg, near_got)
    sums = [z_shift(x, s) for x, s in zip(far_out, FAR)] + [z_shift(x, s) for x, s in zip(near_out, NEAR[1:])]
    back, grads, dz = call(
        dense_kernel,
        (shape((n, BLK), bf16), shape((N_AX, 2 * PIECE, BLK), bf16), shape(cotangent.shape, bf16)),
        (),
        product_flops,
        adj.size,
    )(in_specs=[VMEM] * (6 + len(sums)), out_specs=(VMEM,) * 3)(own, own_deg, *sums, features, cotangent, w_self, w_neigh)

    grads = exchange(grads, "row")
    pair = jnp.stack([back, z_shift(back, 4)])
    shards = call(stack_kernel, shape((Z, n, BLK), bf16), (), adj.size, adj.size)(in_specs=[VMEM] * 5, out_specs=VMEM)(
        pair, z_shift(pair, 1), z_shift(pair, 7), z_shift(back, 2), z_shift(back, 6)
    )
    shards2 = lax.ppermute(shards, "col", SWAP)
    grads = call(spread_kernel, shape(grads.shape, bf16), (), adj.size, adj.size)(
        in_specs=[VMEM, ANY], out_specs=VMEM
    )(grads, shards)
    grads = exchange(grads, "col")
    piece = call(piece_kernel, shape((PIECE, BLK), bf16), (), adj.size, adj.size)(in_specs=[VMEM], out_specs=VMEM)(grads)
    piece2 = lax.ppermute(piece, "row", SWAP)

    keep, send = call(
        adjoint_kernel,
        (shape((HALF, n, width), f32), shape((HALF, n, width), bf16)),
        [stripe, sums_acc],
        product_flops,
        adj.size * 4,
    )(in_specs=[SMEM] * 4 + [VMEM] * 3 + [ANY], out_specs=(VMEM,) * 2)(
        place, block_count, rows, cols, adj, shards, shards2, piece
    )
    send = lax.ppermute(send, "row", SWAP)
    merged = call(
        merge_kernel,
        shape((HALF, n + 2 * PIECE, BLK), bf16),
        [pltpu.VMEM((2, PIECE, BLK), bf16)],
        adj.size,
        adj.size,
    )(in_specs=[SMEM] + [VMEM] * 4, out_specs=VMEM)(place, keep, send, piece, piece2)
    merged = exchange(merged, "row", SAME_CORE)
    scale = (n * N_AX * N_AX) ** (-0.5)
    return call(
        functools.partial(final_kernel, scale),
        (shape((n, width), f32), shape(w_self.shape, f32), shape(w_neigh.shape, f32)),
        (),
        product_flops // 8,
        adj.size,
    )(in_specs=[VMEM] * 3, out_specs=(VMEM,) * 3)(merged, dz, w_self)


def solution(mesh):
    placed = (
        P(("row", "col"), None),
        P(("row", "col"), None),
        P(),
        P(),
        P("row", "col", None, None, None),
        P("row", "col", None),
        P("row", "col", None),
        P("row", "col"),
    )
    return jax.shard_map(
        local,
        mesh=mesh,
        in_specs=placed,
        out_specs=(P(("row", "col"), None), P(), P()),
        check_vma=False,
    )
```

```python
import functools

import jax
import jax.numpy as jnp
from jax import lax
from jax.experimental import pallas as pl
from jax.experimental.pallas import tpu as pltpu
from jax.sharding import PartitionSpec as P

BLK = 128
N_AX = 16
BPD = 2
STRIPE = N_AX * BPD
UNROLL = 20
PIECE = 32
TAIL = 16
HALF = N_AX // 2
Z = 8
NEAR = (0, 2, 6, 1, 7)
FAR = (4, 3, 5)
SHIFTS = (0, 4, 1, 5, 7, 3, 2, 6)
f32 = jnp.float32
bf16 = jnp.bfloat16

VMEM = pl.BlockSpec(memory_space=pltpu.VMEM)
ANY = pl.BlockSpec(memory_space=pl.ANY)
SMEM = pl.BlockSpec(memory_space=pltpu.SMEM)
PARAMS = pltpu.CompilerParams(vmem_limit_bytes=24 * 1024 * 1024)


def dot(a, b, contract=((1,), (0,))):
    return lax.dot_general(a, b, (contract, ((), ())), preferred_element_type=f32)


def slots_loop(count_ref, index_ref, acc_ref, product):
    acc_ref[...] = jnp.zeros_like(acc_ref)
    count = count_ref[0, 0]

    def group(g, carry):
        base = g * UNROLL
        terms = [product(base + u) for u in range(UNROLL)]
        for u in range(UNROLL):
            k = base + u
            at = jnp.where(k < count, index_ref[0, k], STRIPE)
            acc_ref[at] += terms[u]
        return carry

    lax.fori_loop(0, (count + UNROLL - 1) // UNROLL, group, 0)


def wide(x):
    high = x.astype(bf16)
    return jnp.concatenate([high.astype(f32), x - high.astype(f32)], axis=0).astype(bf16)


def degree_kernel(count_ref, rows_ref, adj_ref, out_ref, acc_ref):
    ones = jnp.ones((8, BLK), bf16)
    slots_loop(count_ref, rows_ref, acc_ref, lambda k: dot(ones, adj_ref[k], ((1,), (1,))))
    for d in range(N_AX):
        parts = [acc_ref[d * BPD + b][0:1] for b in range(BPD)]
        out_ref[d] = jnp.concatenate(parts + [jnp.zeros((8 - BPD, BLK), f32)], axis=0)


def tail_of(degree):
    low = degree - degree.astype(bf16).astype(f32)
    parts = [degree[:BPD], low[:BPD], jnp.zeros((TAIL - 2 * BPD, BLK), f32)]
    return jnp.concatenate(parts, axis=0).astype(bf16)


def degree_of(tail):
    tail = tail.astype(f32)
    return jnp.concatenate([tail[:BPD] + tail[BPD : 2 * BPD], jnp.zeros((8 - BPD, BLK), f32)], axis=0)


def forward_kernel(
    place_ref, count_ref, rows_ref, cols_ref, adj_ref, mine_ref, other_ref, deg_ref,
    near_ref, far_ref, near_deg_ref, far_deg_ref, near_send_ref, far_send_ref, x_ref, acc_ref,
):
    core, z, yl = place_ref[0], place_ref[1], place_ref[2]
    for p in range(HALF):
        x_ref[2 * p + core] = mine_ref[p]
        x_ref[2 * p + 1 - core] = other_ref[p]

    def product(k):
        col = cols_ref[0, k]
        at = pl.multiple_of((col % BPD) * BLK, BLK)
        return dot(adj_ref[k], x_ref[col // BPD, pl.ds(at, BLK), :])

    slots_loop(count_ref, rows_ref, acc_ref, product)
    n = BPD * BLK
    for keep, degree, send, shifts in (
        (far_ref, far_deg_ref, far_send_ref, FAR),
        (near_ref, near_deg_ref, near_send_ref, NEAR),
    ):
        for j, s in enumerate(shifts):
            at = 2 * ((z + s) % Z)
            here, there = at + yl, at + 1 - yl
            for b in range(BPD):
                keep[j, b * BLK : (b + 1) * BLK, :] = acc_ref[here * BPD + b]
                send[j, b * BLK : (b + 1) * BLK, :] = acc_ref[there * BPD + b].astype(bf16)
            degree[j] = deg_ref[here]
            send[j, n:, :] = tail_of(deg_ref[there])


def gate_kernel(x_ref, after_ref, out_ref):
    pass


def pair_kernel(keep_ref, deg_ref, got_ref, *out_refs):
    n = BPD * BLK
    first = len(out_refs) - keep_ref.shape[0]
    if first:
        own_ref, own_deg_ref, *out_refs = out_refs
        own_ref[...] = keep_ref[0] + got_ref[0, :n, :].astype(f32)
        own_deg_ref[...] = deg_ref[0] + degree_of(got_ref[0, n:, :])
    for j, out_ref in enumerate(out_refs, first):
        out_ref[:n, :] = (keep_ref[j] + got_ref[j, :n, :].astype(f32)).astype(bf16)
        out_ref[n:, :] = tail_of(deg_ref[j] + degree_of(got_ref[j, n:, :]))


def narrow(parts):
    total = parts[0].astype(f32)
    for d in range(1, parts.shape[0]):
        total += parts[d].astype(f32)
    return total[:PIECE] + total[PIECE:]


def dense_kernel(own_ref, own_deg_ref, *refs):
    *got_refs, x_ref, cot_ref, ws_ref, wn_ref, back_ref, grads_ref, dz_ref = refs
    n = BPD * BLK
    total = own_ref[...]
    degree = own_deg_ref[...]
    for got_ref in got_refs:
        total += got_ref[:n, :].astype(f32)
        degree += degree_of(got_ref[n:, :])
    norm_lanes = lax.rsqrt(1.0 + degree)
    norm = jnp.concatenate(
        [jnp.transpose(jnp.broadcast_to(norm_lanes[b : b + 1], (BLK, BLK))) for b in range(BPD)], axis=0
    )
    agg = (total * norm).astype(bf16)
    x = x_ref[...]
    pre = dot(x, ws_ref[...]) + dot(agg, wn_ref[...])
    sig = jax.nn.sigmoid(pre)
    dz = (cot_ref[...].astype(f32) * (sig * (1.0 + pre * (1.0 - sig)))).astype(bf16)
    dz_ref[...] = dz
    ds = dot(dz, wn_ref[...], ((1,), (1,))) * norm
    for b in range(BPD):
        back_ref[b * BLK : (b + 1) * BLK, :] = jnp.transpose(ds[b * BLK : (b + 1) * BLK]).astype(bf16)
    grads = jnp.concatenate([dot(x, dz, ((0,), (0,))), dot(agg, dz, ((0,), (0,)))], axis=0)
    pieces = jnp.concatenate([grads[:, :BLK], grads[:, BLK:]], axis=0)
    for d in range(N_AX):
        grads_ref[d] = wide(pieces[d * PIECE : (d + 1) * PIECE])


def stack_kernel(*refs):
    *parts, _, out_ref = refs
    at = 0
    for part in parts:
        count = part.shape[0] if len(part.shape) == 3 else 1
        out_ref[at : at + count] = part[...].reshape(count, *out_ref.shape[1:])
        at += count


def row_kernel(got_ref, out_ref):
    out_ref[...] = wide(narrow(got_ref))


def spread_kernel(mine_ref, other_ref, after_ref, out_ref):
    total = mine_ref[...].astype(f32) + other_ref[...].astype(f32)
    total = wide(total[:PIECE] + total[PIECE:])
    for d in range(out_ref.shape[0]):
        out_ref[d] = total


def piece_kernel(got_ref, out_ref):
    out_ref[...] = narrow(got_ref).astype(bf16)


def adjoint_kernel(
    place_ref, count_ref, rows_ref, cols_ref, adj_ref, mine_ref, other_ref, after_ref, keep_ref, send_ref, x_ref, acc_ref
):
    z, yl = place_ref[1], place_ref[2]
    for j, s in enumerate(SHIFTS):
        at = 2 * ((z + Z - s) % Z)
        x_ref[at + yl] = mine_ref[j]
        x_ref[at + 1 - yl] = other_ref[j]

    def product(k):
        row = rows_ref[0, k]
        at = pl.multiple_of((row % BPD) * BLK, BLK)
        return dot(x_ref[row // BPD, pl.ds(at, BLK), :], adj_ref[k])

    slots_loop(count_ref, cols_ref, acc_ref, product)
    core = place_ref[0]
    n = BPD * BLK
    for p in range(HALF):
        for b in range(BPD):
            keep_ref[p, b * BLK : (b + 1) * BLK, :] = acc_ref[(2 * p + core) * BPD + b]
            send_ref[p, b * BLK : (b + 1) * BLK, :] = acc_ref[(2 * p + 1 - core) * BPD + b].astype(bf16)


def merge_kernel(place_ref, keep_ref, got_ref, piece_ref, piece2_ref, out_ref, both_ref):
    n = BPD * BLK
    core = place_ref[0]
    both_ref[core] = piece_ref[...]
    both_ref[1 - core] = piece2_ref[...]
    for p in range(HALF):
        out_ref[p, :n, :] = (keep_ref[p] + got_ref[p].astype(f32)).astype(bf16)
        for c in range(2):
            out_ref[p, n + c * PIECE : n + (c + 1) * PIECE, :] = both_ref[c]


def final_kernel(scale, got_ref, dz_ref, ws_ref, out_ref, self_ref, neigh_ref):
    n = BPD * BLK
    total = got_ref[0, :n, :].astype(f32)
    for d in range(1, HALF):
        total += got_ref[d, :n, :].astype(f32)
    adjoint = jnp.concatenate([jnp.transpose(total[b * BLK : (b + 1) * BLK]) for b in range(BPD)], axis=0)
    out_ref[...] = dot(dz_ref[...], ws_ref[...], ((1,), (1,))) + adjoint
    per = BLK // (2 * PIECE)
    for d in range(HALF):
        quarter, at = d // per, (d % per) * 2 * PIECE
        lanes = (quarter // 2) * BLK
        into = neigh_ref if quarter % 2 else self_ref
        into[at : at + 2 * PIECE, lanes : lanes + BLK] = got_ref[d, n:, :].astype(f32) * scale


def call(kernel, out, scratch=(), flops=0, moved=0):
    return functools.partial(
        pl.pallas_call,
        kernel,
        out_shape=out,
        scratch_shapes=list(scratch),
        compiler_params=PARAMS,
        cost_estimate=pl.CostEstimate(flops=flops, bytes_accessed=moved, transcendentals=0),
    )


def exchange(x, axis, groups=None):
    return lax.all_to_all(x, axis, 0, 0, axis_index_groups=groups)


SAME_PARITY = [list(range(core, N_AX, 2)) for core in range(2)]
SWAP = [(i, i ^ 1) for i in range(N_AX)]


def z_shift(x, s):
    return lax.ppermute(x, "col", [(i, (i + 2 * s) % N_AX) for i in range(N_AX)])


def local(features, cotangent, w_self, w_neigh, adj_blocks, block_rows, block_cols, block_count):
    adj = adj_blocks[0, 0]
    rows = block_rows[0]
    cols = block_cols[0]
    slots = adj.shape[0]
    n, width = features.shape
    product_flops = 2 * slots * BLK**3
    shape = jax.ShapeDtypeStruct
    sums_acc = pltpu.VMEM((STRIPE + 1, BLK, BLK), f32)
    stripe = pltpu.VMEM((N_AX, n, width), bf16)
    row_at, col_at = lax.axis_index("row"), lax.axis_index("col")
    place = jnp.stack([row_at % 2, col_at // 2, col_at % 2]).astype(jnp.int32)

    mine = exchange(jnp.broadcast_to(features[None], (HALF, n, width)), "row", SAME_PARITY)
    degree = call(
        degree_kernel,
        shape((N_AX, 8, BLK), f32),
        [pltpu.VMEM((STRIPE + 1, 8, BLK), f32)],
        product_flops // 16,
        adj.size * 2,
    )(in_specs=[SMEM, SMEM, VMEM], out_specs=VMEM)(block_count, rows, adj)
    mine, degree = lax.optimization_barrier((mine, degree))
    other = lax.ppermute(mine, "row", SWAP)
    near, far = len(NEAR), len(FAR)
    near_keep, far_keep, near_deg, far_deg, near_send, far_send = call(
        forward_kernel,
        (
            shape((near, n, BLK), f32),
            shape((far, n, BLK), f32),
            shape((near, 8, BLK), f32),
            shape((far, 8, BLK), f32),
            shape((near, n + TAIL, BLK), bf16),
            shape((far, n + TAIL, BLK), bf16),
        ),
        [stripe, sums_acc],
        product_flops,
        adj.size * 4,
    )(in_specs=[SMEM] * 4 + [VMEM] * 4, out_specs=(VMEM,) * 6)(
        place, block_count, rows, cols, adj, mine, other, degree
    )
    far_got = lax.ppermute(far_send, "col", SWAP)
    near_send = call(gate_kernel, shape(near_send.shape, bf16))(
        in_specs=[ANY, ANY], out_specs=ANY, input_output_aliases={0: 0}
    )(near_send, far_got)
    near_got = lax.ppermute(near_send, "col", SWAP)
    block = shape((n + TAIL, BLK), bf16)
    far_out = call(pair_kernel, (block,) * far, (), adj.size, adj.size)(
        in_specs=[VMEM] * 3, out_specs=(VMEM,) * far
    )(far_keep, far_deg, far_got)
    own, own_deg, *near_out = call(
        pair_kernel, (shape((n, BLK), f32), shape((8, BLK), f32)) + (block,) * (near - 1), (), adj.size, adj.size
    )(in_specs=[VMEM] * 3, out_specs=(VMEM,) * (near + 1))(near_keep, near_deg, near_got)
    sums = [z_shift(x, s) for x, s in zip(far_out, FAR)] + [z_shift(x, s) for x, s in zip(near_out, NEAR[1:])]
    back, grads, dz = call(
        dense_kernel,
        (shape((n, BLK), bf16), shape((N_AX, 2 * PIECE, BLK), bf16), shape(cotangent.shape, bf16)),
        (),
        product_flops,
        adj.size,
    )(in_specs=[VMEM] * (6 + len(sums)), out_specs=(VMEM,) * 3)(own, own_deg, *sums, features, cotangent, w_self, w_neigh)

    grads = exchange(grads, "row")
    pair = jnp.stack([back, z_shift(back, 4)])
    part = call(row_kernel, shape((2 * PIECE, BLK), bf16), (), adj.size, adj.size)(in_specs=[VMEM], out_specs=VMEM)(grads)
    part2 = lax.ppermute(part, "col", SWAP)
    shards = call(stack_kernel, shape((Z, n, BLK), bf16), (), adj.size, adj.size)(in_specs=[VMEM] * 5 + [ANY], out_specs=VMEM)(
        pair, z_shift(pair, 1), z_shift(pair, 7), z_shift(back, 2), z_shift(back, 6), part2
    )
    shards2 = lax.ppermute(shards, "col", SWAP)
    grads = call(spread_kernel, shape((Z, 2 * PIECE, BLK), bf16), (), adj.size, adj.size)(
        in_specs=[VMEM] * 2 + [ANY], out_specs=VMEM
    )(part, part2, shards)
    grads = exchange(grads, "col", SAME_PARITY)
    piece = call(piece_kernel, shape((PIECE, BLK), bf16), (), adj.size, adj.size)(in_specs=[VMEM], out_specs=VMEM)(grads)
    piece2 = lax.ppermute(piece, "row", SWAP)

    keep, send = call(
        adjoint_kernel,
        (shape((HALF, n, width), f32), shape((HALF, n, width), bf16)),
        [stripe, sums_acc],
        product_flops,
        adj.size * 4,
    )(in_specs=[SMEM] * 4 + [VMEM] * 3 + [ANY], out_specs=(VMEM,) * 2)(
        place, block_count, rows, cols, adj, shards, shards2, piece
    )
    send = lax.ppermute(send, "row", SWAP)
    merged = call(
        merge_kernel,
        shape((HALF, n + 2 * PIECE, BLK), bf16),
        [pltpu.VMEM((2, PIECE, BLK), bf16)],
        adj.size,
        adj.size,
    )(in_specs=[SMEM] + [VMEM] * 4, out_specs=VMEM)(place, keep, send, piece, piece2)
    merged = exchange(merged, "row", SAME_PARITY)
    scale = (n * N_AX * N_AX) ** (-0.5)
    return call(
        functools.partial(final_kernel, scale),
        (shape((n, width), f32), shape(w_self.shape, f32), shape(w_neigh.shape, f32)),
        (),
        product_flops // 8,
        adj.size,
    )(in_specs=[VMEM] * 3, out_specs=(VMEM,) * 3)(merged, dz, w_self)


def solution(mesh):
    placed = (
        P(("row", "col"), None),
        P(("row", "col"), None),
        P(),
        P(),
        P("row", "col", None, None, None),
        P("row", "col", None),
        P("row", "col", None),
        P("row", "col"),
    )
    return jax.shard_map(
        local,
        mesh=mesh,
        in_specs=placed,
        out_specs=(P(("row", "col"), None), P(), P()),
        check_vma=False,
    )
```

```python
import functools

import jax
import jax.numpy as jnp
from jax import lax
from jax.experimental import pallas as pl
from jax.experimental.pallas import tpu as pltpu
from jax.sharding import PartitionSpec as P

BLK = 128
N_AX = 16
BPD = 2
STRIPE = N_AX * BPD
UNROLL = 40
PIECE = 32
TAIL = 16
HALF = N_AX // 2
Z = 8
NEAR = (0, 2, 6, 1, 7)
FAR = (4, 3, 5)
SHIFTS = (0, 4, 1, 5, 7, 3, 2, 6)
f32 = jnp.float32
bf16 = jnp.bfloat16

VMEM = pl.BlockSpec(memory_space=pltpu.VMEM)
ANY = pl.BlockSpec(memory_space=pl.ANY)
SMEM = pl.BlockSpec(memory_space=pltpu.SMEM)
PARAMS = pltpu.CompilerParams(vmem_limit_bytes=24 * 1024 * 1024)


def dot(a, b, contract=((1,), (0,))):
    return lax.dot_general(a, b, (contract, ((), ())), preferred_element_type=f32)


def slots_loop(count_ref, index_ref, acc_ref, product):
    acc_ref[...] = jnp.zeros_like(acc_ref)
    count = count_ref[0, 0]

    def group(g, carry):
        base = g * UNROLL
        terms = [product(base + u) for u in range(UNROLL)]
        for u in range(UNROLL):
            k = base + u
            at = jnp.where(k < count, index_ref[0, k], STRIPE)
            acc_ref[at] += terms[u]
        return carry

    lax.fori_loop(0, (count + UNROLL - 1) // UNROLL, group, 0)


def wide(x):
    high = x.astype(bf16)
    return jnp.concatenate([high.astype(f32), x - high.astype(f32)], axis=0).astype(bf16)


def degree_kernel(count_ref, rows_ref, adj_ref, out_ref, acc_ref):
    ones = jnp.ones((8, BLK), bf16)
    slots_loop(count_ref, rows_ref, acc_ref, lambda k: dot(ones, adj_ref[k], ((1,), (1,))))
    for d in range(N_AX):
        parts = [acc_ref[d * BPD + b][0:1] for b in range(BPD)]
        out_ref[d] = jnp.concatenate(parts + [jnp.zeros((8 - BPD, BLK), f32)], axis=0)


def tail_of(degree):
    low = degree - degree.astype(bf16).astype(f32)
    parts = [degree[:BPD], low[:BPD], jnp.zeros((TAIL - 2 * BPD, BLK), f32)]
    return jnp.concatenate(parts, axis=0).astype(bf16)


def degree_of(tail):
    tail = tail.astype(f32)
    return jnp.concatenate([tail[:BPD] + tail[BPD : 2 * BPD], jnp.zeros((8 - BPD, BLK), f32)], axis=0)


def forward_kernel(
    place_ref, count_ref, rows_ref, cols_ref, adj_ref, mine_ref, other_ref, deg_ref,
    near_ref, far_ref, near_deg_ref, far_deg_ref, near_send_ref, far_send_ref, x_ref, acc_ref,
):
    core, z, yl = place_ref[0], place_ref[1], place_ref[2]
    for p in range(HALF):
        x_ref[2 * p + core] = mine_ref[p]
        x_ref[2 * p + 1 - core] = other_ref[p]

    def product(k):
        col = cols_ref[0, k]
        at = pl.multiple_of((col % BPD) * BLK, BLK)
        return dot(adj_ref[k], x_ref[col // BPD, pl.ds(at, BLK), :])

    slots_loop(count_ref, rows_ref, acc_ref, product)
    n = BPD * BLK
    for keep, degree, send, shifts in (
        (far_ref, far_deg_ref, far_send_ref, FAR),
        (near_ref, near_deg_ref, near_send_ref, NEAR),
    ):
        for j, s in enumerate(shifts):
            at = 2 * ((z + s) % Z)
            here, there = at + yl, at + 1 - yl
            for b in range(BPD):
                keep[j, b * BLK : (b + 1) * BLK, :] = acc_ref[here * BPD + b]
                send[j, b * BLK : (b + 1) * BLK, :] = acc_ref[there * BPD + b].astype(bf16)
            degree[j] = deg_ref[here]
            send[j, n:, :] = tail_of(deg_ref[there])


def gate_kernel(x_ref, after_ref, out_ref):
    pass


def pair_kernel(keep_ref, deg_ref, got_ref, *out_refs):
    n = BPD * BLK
    first = len(out_refs) - keep_ref.shape[0]
    if first:
        own_ref, own_deg_ref, *out_refs = out_refs
        own_ref[...] = keep_ref[0] + got_ref[0, :n, :].astype(f32)
        own_deg_ref[...] = deg_ref[0] + degree_of(got_ref[0, n:, :])
    for j, out_ref in enumerate(out_refs, first):
        out_ref[:n, :] = (keep_ref[j] + got_ref[j, :n, :].astype(f32)).astype(bf16)
        out_ref[n:, :] = tail_of(deg_ref[j] + degree_of(got_ref[j, n:, :]))


def narrow(parts):
    total = parts[0].astype(f32)
    for d in range(1, parts.shape[0]):
        total += parts[d].astype(f32)
    return total[:PIECE] + total[PIECE:]


def dense_kernel(own_ref, own_deg_ref, *refs):
    *got_refs, x_ref, cot_ref, ws_ref, wn_ref, back_ref, grads_ref, dz_ref = refs
    n = BPD * BLK
    total = own_ref[...]
    degree = own_deg_ref[...]
    for got_ref in got_refs:
        total += got_ref[:n, :].astype(f32)
        degree += degree_of(got_ref[n:, :])
    norm_lanes = lax.rsqrt(1.0 + degree)
    norm = jnp.concatenate(
        [jnp.transpose(jnp.broadcast_to(norm_lanes[b : b + 1], (BLK, BLK))) for b in range(BPD)], axis=0
    )
    agg = (total * norm).astype(bf16)
    x = x_ref[...]
    pre = dot(x, ws_ref[...]) + dot(agg, wn_ref[...])
    sig = jax.nn.sigmoid(pre)
    dz = (cot_ref[...].astype(f32) * (sig * (1.0 + pre * (1.0 - sig)))).astype(bf16)
    dz_ref[...] = dz
    ds = dot(dz, wn_ref[...], ((1,), (1,))) * norm
    for b in range(BPD):
        back_ref[b * BLK : (b + 1) * BLK, :] = jnp.transpose(ds[b * BLK : (b + 1) * BLK]).astype(bf16)
    grads = jnp.concatenate([dot(x, dz, ((0,), (0,))), dot(agg, dz, ((0,), (0,)))], axis=0)
    pieces = jnp.concatenate([grads[:, :BLK], grads[:, BLK:]], axis=0)
    for d in range(N_AX):
        grads_ref[d] = wide(pieces[d * PIECE : (d + 1) * PIECE])


def stack_kernel(*refs):
    *parts, _, out_ref = refs
    at = 0
    for part in parts:
        count = part.shape[0] if len(part.shape) == 3 else 1
        out_ref[at : at + count] = part[...].reshape(count, *out_ref.shape[1:])
        at += count


def row_kernel(got_ref, out_ref):
    out_ref[...] = wide(narrow(got_ref))


def spread_kernel(mine_ref, other_ref, after_ref, out_ref):
    total = mine_ref[...].astype(f32) + other_ref[...].astype(f32)
    total = wide(total[:PIECE] + total[PIECE:])
    for d in range(out_ref.shape[0]):
        out_ref[d] = total


def piece_kernel(got_ref, out_ref):
    out_ref[...] = narrow(got_ref).astype(bf16)


def adjoint_kernel(
    place_ref, count_ref, rows_ref, cols_ref, adj_ref, mine_ref, other_ref, after_ref, keep_ref, send_ref, x_ref, acc_ref
):
    z, yl = place_ref[1], place_ref[2]
    for j, s in enumerate(SHIFTS):
        at = 2 * ((z + Z - s) % Z)
        x_ref[at + yl] = mine_ref[j]
        x_ref[at + 1 - yl] = other_ref[j]

    def product(k):
        row = rows_ref[0, k]
        at = pl.multiple_of((row % BPD) * BLK, BLK)
        return dot(x_ref[row // BPD, pl.ds(at, BLK), :], adj_ref[k])

    slots_loop(count_ref, cols_ref, acc_ref, product)
    core = place_ref[0]
    n = BPD * BLK
    for p in range(HALF):
        for b in range(BPD):
            keep_ref[p, b * BLK : (b + 1) * BLK, :] = acc_ref[(2 * p + core) * BPD + b]
            send_ref[p, b * BLK : (b + 1) * BLK, :] = acc_ref[(2 * p + 1 - core) * BPD + b].astype(bf16)


def merge_kernel(place_ref, keep_ref, got_ref, piece_ref, piece2_ref, out_ref, both_ref):
    n = BPD * BLK
    core = place_ref[0]
    both_ref[core] = piece_ref[...]
    both_ref[1 - core] = piece2_ref[...]
    for p in range(HALF):
        out_ref[p, :n, :] = (keep_ref[p] + got_ref[p].astype(f32)).astype(bf16)
        for c in range(2):
            out_ref[p, n + c * PIECE : n + (c + 1) * PIECE, :] = both_ref[c]


def final_kernel(scale, got_ref, dz_ref, ws_ref, out_ref, self_ref, neigh_ref):
    n = BPD * BLK
    total = got_ref[0, :n, :].astype(f32)
    for d in range(1, HALF):
        total += got_ref[d, :n, :].astype(f32)
    adjoint = jnp.concatenate([jnp.transpose(total[b * BLK : (b + 1) * BLK]) for b in range(BPD)], axis=0)
    out_ref[...] = dot(dz_ref[...], ws_ref[...], ((1,), (1,))) + adjoint
    per = BLK // (2 * PIECE)
    for d in range(HALF):
        quarter, at = d // per, (d % per) * 2 * PIECE
        lanes = (quarter // 2) * BLK
        into = neigh_ref if quarter % 2 else self_ref
        into[at : at + 2 * PIECE, lanes : lanes + BLK] = got_ref[d, n:, :].astype(f32) * scale


def call(kernel, out, scratch=(), flops=0, moved=0):
    return functools.partial(
        pl.pallas_call,
        kernel,
        out_shape=out,
        scratch_shapes=list(scratch),
        compiler_params=PARAMS,
        cost_estimate=pl.CostEstimate(flops=flops, bytes_accessed=moved, transcendentals=0),
    )


def exchange(x, axis, groups=None):
    return lax.all_to_all(x, axis, 0, 0, axis_index_groups=groups)


SAME_PARITY = [list(range(core, N_AX, 2)) for core in range(2)]
SWAP = [(i, i ^ 1) for i in range(N_AX)]


def z_shift(x, s):
    return lax.ppermute(x, "col", [(i, (i + 2 * s) % N_AX) for i in range(N_AX)])


def local(features, cotangent, w_self, w_neigh, adj_blocks, block_rows, block_cols, block_count):
    adj = adj_blocks[0, 0]
    rows = block_rows[0]
    cols = block_cols[0]
    slots = adj.shape[0]
    n, width = features.shape
    product_flops = 2 * slots * BLK**3
    shape = jax.ShapeDtypeStruct
    sums_acc = pltpu.VMEM((STRIPE + 1, BLK, BLK), f32)
    stripe = pltpu.VMEM((N_AX, n, width), bf16)
    row_at, col_at = lax.axis_index("row"), lax.axis_index("col")
    place = jnp.stack([row_at % 2, col_at // 2, col_at % 2]).astype(jnp.int32)

    mine = exchange(jnp.broadcast_to(features[None], (HALF, n, width)), "row", SAME_PARITY)
    degree = call(
        degree_kernel,
        shape((N_AX, 8, BLK), f32),
        [pltpu.VMEM((STRIPE + 1, 8, BLK), f32)],
        product_flops // 16,
        adj.size * 2,
    )(in_specs=[SMEM, SMEM, VMEM], out_specs=VMEM)(block_count, rows, adj)
    mine, degree = lax.optimization_barrier((mine, degree))
    other = lax.ppermute(mine, "row", SWAP)
    near, far = len(NEAR), len(FAR)
    near_keep, far_keep, near_deg, far_deg, near_send, far_send = call(
        forward_kernel,
        (
            shape((near, n, BLK), f32),
            shape((far, n, BLK), f32),
            shape((near, 8, BLK), f32),
            shape((far, 8, BLK), f32),
            shape((near, n + TAIL, BLK), bf16),
            shape((far, n + TAIL, BLK), bf16),
        ),
        [stripe, sums_acc],
        product_flops,
        adj.size * 4,
    )(in_specs=[SMEM] * 4 + [VMEM] * 4, out_specs=(VMEM,) * 6)(
        place, block_count, rows, cols, adj, mine, other, degree
    )
    far_got = lax.ppermute(far_send, "col", SWAP)
    near_send = call(gate_kernel, shape(near_send.shape, bf16))(
        in_specs=[ANY, ANY], out_specs=ANY, input_output_aliases={0: 0}
    )(near_send, far_got)
    near_got = lax.ppermute(near_send, "col", SWAP)
    block = shape((n + TAIL, BLK), bf16)
    far_out = call(pair_kernel, (block,) * far, (), adj.size, adj.size)(
        in_specs=[VMEM] * 3, out_specs=(VMEM,) * far
    )(far_keep, far_deg, far_got)
    own, own_deg, *near_out = call(
        pair_kernel, (shape((n, BLK), f32), shape((8, BLK), f32)) + (block,) * (near - 1), (), adj.size, adj.size
    )(in_specs=[VMEM] * 3, out_specs=(VMEM,) * (near + 1))(near_keep, near_deg, near_got)
    sums = [z_shift(x, s) for x, s in zip(far_out, FAR)] + [z_shift(x, s) for x, s in zip(near_out, NEAR[1:])]
    back, grads, dz = call(
        dense_kernel,
        (shape((n, BLK), bf16), shape((N_AX, 2 * PIECE, BLK), bf16), shape(cotangent.shape, bf16)),
        (),
        product_flops,
        adj.size,
    )(in_specs=[VMEM] * (6 + len(sums)), out_specs=(VMEM,) * 3)(own, own_deg, *sums, features, cotangent, w_self, w_neigh)

    grads = exchange(grads, "row")
    pair = jnp.stack([back, z_shift(back, 4)])
    part = call(row_kernel, shape((2 * PIECE, BLK), bf16), (), adj.size, adj.size)(in_specs=[VMEM], out_specs=VMEM)(grads)
    part2 = lax.ppermute(part, "col", SWAP)
    shards = call(stack_kernel, shape((Z, n, BLK), bf16), (), adj.size, adj.size)(in_specs=[VMEM] * 5 + [ANY], out_specs=VMEM)(
        pair, z_shift(pair, 1), z_shift(pair, 7), z_shift(back, 2), z_shift(back, 6), part2
    )
    shards2 = lax.ppermute(shards, "col", SWAP)
    grads = call(spread_kernel, shape((Z, 2 * PIECE, BLK), bf16), (), adj.size, adj.size)(
        in_specs=[VMEM] * 2 + [ANY], out_specs=VMEM
    )(part, part2, shards)
    grads = exchange(grads, "col", SAME_PARITY)
    piece = call(piece_kernel, shape((PIECE, BLK), bf16), (), adj.size, adj.size)(in_specs=[VMEM], out_specs=VMEM)(grads)
    piece2 = lax.ppermute(piece, "row", SWAP)

    keep, send = call(
        adjoint_kernel,
        (shape((HALF, n, width), f32), shape((HALF, n, width), bf16)),
        [stripe, sums_acc],
        product_flops,
        adj.size * 4,
    )(in_specs=[SMEM] * 4 + [VMEM] * 3 + [ANY], out_specs=(VMEM,) * 2)(
        place, block_count, rows, cols, adj, shards, shards2, piece
    )
    send = lax.ppermute(send, "row", SWAP)
    merged = call(
        merge_kernel,
        shape((HALF, n + 2 * PIECE, BLK), bf16),
        [pltpu.VMEM((2, PIECE, BLK), bf16)],
        adj.size,
        adj.size,
    )(in_specs=[SMEM] + [VMEM] * 4, out_specs=VMEM)(place, keep, send, piece, piece2)
    merged = exchange(merged, "row", SAME_PARITY)
    scale = (n * N_AX * N_AX) ** (-0.5)
    return call(
        functools.partial(final_kernel, scale),
        (shape((n, width), f32), shape(w_self.shape, f32), shape(w_neigh.shape, f32)),
        (),
        product_flops // 8,
        adj.size,
    )(in_specs=[VMEM] * 3, out_specs=(VMEM,) * 3)(merged, dz, w_self)


def solution(mesh):
    placed = (
        P(("row", "col"), None),
        P(("row", "col"), None),
        P(),
        P(),
        P("row", "col", None, None, None),
        P("row", "col", None),
        P("row", "col", None),
        P("row", "col"),
    )
    return jax.shard_map(
        local,
        mesh=mesh,
        in_specs=placed,
        out_specs=(P(("row", "col"), None), P(), P()),
        check_vma=False,
    )
```
